512 devices in a mesh: group: 8 (over y, core), dev: 64 (over z, x).
Axes of the slice: x: 4, y: 4, z: 16, core: 2. Of those that a mesh axis runs over, the one named last changes fastest.
Arguments:
- level_set: bfloat16 [2048, 64, 64, 64], P(('group', 'dev')), may hold values from -6 to 6
- node_coords: float32 [3, 2048, 512], P(None, ('group', 'dev')), may hold values from -5 to 5
- position: float32 [3, 2048], P(None, ('group', 'dev')), may hold values from -2 to 2
- quaternion: float32 [4, 2048], P(None, ('group', 'dev')), may hold values from -1 to 1, as said below
- velocity: float32 [3, 2048], P(None, ('group', 'dev')), may hold values from -3 to 3
- spin: float32 [3, 2048], P(None, ('group', 'dev')), may hold values from -1.8 to 1.8
- mass: float32 [2048], P(('group', 'dev')), may hold values from 0.5 to 2
- grid_slot: int32 [65536], P(('group', 'dev')), may hold values from 0 to 3
- brick_anchor: int32 [3, 65536], P(None, ('group', 'dev')), may hold values from 27 to 29
- node_slot: int32 [65536], P(('group', 'dev')), may hold values from -1 to 3, as said below
- grid_cross: int32 [8192], P(('group', 'dev')), may hold values from 0 to 3
- anchor_cross: int32 [3, 8192], P(None, ('group', 'dev')), may hold values from 27 to 29
- node_cross: int32 [8192], P(('group', 'dev')), may hold values from -1 to 3, as said below
Outputs:
- new_position: float32 [3, 2048], P(None, ('group', 'dev'))
- new_quaternion: float32 [4, 2048], P(None, ('group', 'dev'))
- new_velocity: float32 [3, 2048], P(None, ('group', 'dev'))
- new_spin: float32 [3, 2048], P(None, ('group', 'dev'))
The draws below stay inside these ranges and needn't reach their ends.
Inputs may be any that keep to these rules, and one draw needn't show every extreme that they name: Each column is a unit quaternion. `node_slot`: -1 marks a slot without a pair; the slot correspondence is the one of the step that defines pairs. `node_cross`: -1 marks a slot without a pair; every entry of the first group is -1.
All inputs are finite; a program needn't handle non-finite values.
Results may differ from the reference program's by a relative error of at most 0.0009.
Values may be sent and summed in bfloat16 or wider, within the bound.
A program may use at most 64 MiB of HBM per device.

```python
import math
import jax
import jax.numpy as jnp
from jax import lax

GRID = 64
NODES = 512
BRICK = 8
GRAINS_DEV = 4
SLOT_CAP = 2
CROSS_CAP = 16
OWNERS = 512
SLOTS = 128
GRAINS = 2048
N_GROUP = 8
N_DEV = 64


def draw_quaternion(key, part):
    key = jax.random.fold_in(key, 13)
    subkeys = jax.random.split(key, 3)
    half_angle = jax.random.uniform(subkeys[0], (GRAINS,), jnp.float32, 0.0, math.pi)
    axis_cos = jax.random.uniform(subkeys[1], (GRAINS,), jnp.float32, -1.0, 1.0)
    azimuth = jax.random.uniform(subkeys[2], (GRAINS,), jnp.float32, -math.pi, math.pi)
    axis_sin = jnp.sqrt(jnp.maximum(1.0 - axis_cos * axis_cos, 0.0))
    sine_half = jnp.sin(half_angle)
    return jnp.stack([jnp.cos(half_angle), sine_half * axis_sin * jnp.cos(azimuth), sine_half * axis_sin * jnp.sin(azimuth), sine_half * axis_cos]).astype(jnp.float32)


def draw_node_slot(key, part):
    key = jax.random.fold_in(key, 11)
    drawn = jax.random.randint(key, (OWNERS * SLOTS,), 0, 2 * GRAINS_DEV, dtype=jnp.int32)
    return jnp.where(drawn < GRAINS_DEV, drawn, -1).astype(jnp.int32)


def draw_node_cross(key, part):
    key = jax.random.fold_in(key, 12)
    drawn = jax.random.randint(key, (OWNERS * CROSS_CAP,), 0, 2 * GRAINS_DEV, dtype=jnp.int32)
    first_group = jnp.arange(OWNERS * CROSS_CAP, dtype=jnp.int32) < N_DEV * CROSS_CAP
    return jnp.where((drawn < GRAINS_DEV) & jnp.logical_not(first_group), drawn, -1).astype(jnp.int32)


def touch_ends(entries, stream_key, least, top_value):
    dims = entries.shape
    spot = [jax.random.randint(jax.random.fold_in(stream_key, axis), (), 0, dims[axis]) for axis in range(len(dims))]
    entries = entries.at[tuple(spot)].set(least)
    longest = dims.index(max(dims))
    spot[longest] = (spot[longest] + 1) % dims[longest]
    return entries.at[tuple(spot)].set(top_value)


def block_levels(rng, shape, cuts, low, largest):
    def one(dim, parts):
        heights = jax.random.uniform(jax.random.fold_in(jax.random.fold_in(rng, 6), dim), (parts,), jnp.float32, low / len(cuts), largest / len(cuts))
        return jnp.repeat(jnp.exp(heights), shape[dim] // parts).reshape((-1,) + (1,) * (len(shape) - dim - 1))

    loudness = one(*cuts[0])
    for cut in cuts[1:]:
        loudness = loudness * one(*cut)
    return loudness


def normal_values(rng, dims, width, limit, cuts=(), kind=jnp.bfloat16):
    level = block_levels(rng, dims, cuts, -0.22, 0.18) if cuts else 1.0
    values = jax.random.normal(rng, dims, jnp.float32) * width * level
    return jnp.minimum(jnp.maximum(values, -limit), limit).astype(kind)


def setup_inputs(seed: int = 0) -> dict:
    key_of = jax.random.split(jax.random.key(seed), 14)
    return {
        "level_set": normal_values(key_of[0], (GRAINS, GRID, GRID, GRID), 1.0, 6.0, ((0, 512),)),
        "node_coords": jnp.clip(jax.random.uniform(key_of[1], (3, GRAINS, NODES), jnp.float32, -5.0, 5.0) * block_levels(key_of[1], (3, GRAINS, NODES), ((1, 512),), -0.4, 0.0), -5.0, 5.0),
        "position": normal_values(key_of[2], (3, GRAINS), 0.5, 2.0, ((1, 512),), jnp.float32),
        "quaternion": draw_quaternion(jax.random.fold_in(key_of[13], 71), 0),
        "velocity": normal_values(key_of[4], (3, GRAINS), 0.5, 3.0, ((1, 512),), jnp.float32),
        "spin": normal_values(key_of[5], (3, GRAINS), 0.3, 1.8, ((1, 512),), jnp.float32),
        "mass": jnp.clip(jnp.exp(math.log(2.0) - 1.3862944 * jax.random.uniform(key_of[6], (GRAINS,), jnp.float32) ** block_levels(key_of[6], (GRAINS,), ((0, 512),), -0.2, 0.2)), 0.5, 2.0),
        "grid_slot": touch_ends(jax.random.randint(key_of[7], (OWNERS * SLOTS,), 0, GRAINS_DEV), jax.random.fold_in(key_of[7], 1), 0, GRAINS_DEV - 1).astype(jnp.int32),
        "brick_anchor": touch_ends(jax.random.randint(key_of[8], (3, OWNERS * SLOTS), GRID // 2 - 5, GRID // 2 - 2), jax.random.fold_in(key_of[8], 1), GRID // 2 - 5, (GRID // 2 - 2) - 1).astype(jnp.int32),
        "node_slot": draw_node_slot(jax.random.fold_in(key_of[13], 71), 0),
        "grid_cross": touch_ends(jax.random.randint(key_of[10], (OWNERS * CROSS_CAP,), 0, GRAINS_DEV), jax.random.fold_in(key_of[10], 1), 0, GRAINS_DEV - 1).astype(jnp.int32),
        "anchor_cross": touch_ends(jax.random.randint(key_of[11], (3, OWNERS * CROSS_CAP), GRID // 2 - 5, GRID // 2 - 2), jax.random.fold_in(key_of[11], 1), GRID // 2 - 5, (GRID // 2 - 2) - 1).astype(jnp.int32),
        "node_cross": draw_node_cross(jax.random.fold_in(key_of[13], 71), 0),
    }


stiffness = 0.1
time_step = 0.5
spacing = 0.5
highest = lax.Precision.HIGHEST

def rotation(quaternion):
    scalar_q = quaternion[0]
    vec_x = quaternion[1]
    vec_y = quaternion[2]
    vec_z = quaternion[3]
    first_row = jnp.stack([1.0 - 2.0 * (vec_y * vec_y + vec_z * vec_z), 2.0 * (vec_x * vec_y - scalar_q * vec_z), 2.0 * (vec_x * vec_z + scalar_q * vec_y)])
    second_row = jnp.stack([2.0 * (vec_x * vec_y + scalar_q * vec_z), 1.0 - 2.0 * (vec_x * vec_x + vec_z * vec_z), 2.0 * (vec_y * vec_z - scalar_q * vec_x)])
    third_row = jnp.stack([2.0 * (vec_x * vec_z - scalar_q * vec_y), 2.0 * (vec_y * vec_z + scalar_q * vec_x), 1.0 - 2.0 * (vec_x * vec_x + vec_y * vec_y)])
    return jnp.stack([first_row, second_row, third_row])

def hat_weights(brick_coord):
    places = jnp.arange(BRICK).astype(jnp.float32)
    offsets = brick_coord[None, :] - places[:, None]
    center_hat = jnp.maximum(1.0 - jnp.abs(offsets), 0.0)
    upper_hat = jnp.maximum(1.0 - jnp.abs(offsets + spacing), 0.0)
    lower_hat = jnp.maximum(1.0 - jnp.abs(offsets - spacing), 0.0)
    return (center_hat, (upper_hat - lower_hat) / (2.0 * spacing))

def contact(node_arms, centre, brick_vals, anchor, place_j, turn_j):
    world_pos = centre[:, None] + node_arms
    relative = world_pos - place_j[:, None]
    in_frame = jnp.dot(turn_j.T, relative, precision=highest)
    brick_coord = in_frame + (GRID - 1) / 2.0 - anchor[:, None]
    hat_x, slope_x = hat_weights(brick_coord[0])
    hat_y, slope_y = hat_weights(brick_coord[1])
    hat_z, slope_z = hat_weights(brick_coord[2])
    contracted = jnp.einsum('abc,kan->kbcn', brick_vals.astype(jnp.float32), jnp.stack([hat_x, slope_x]), precision=highest)
    value_rows = lax.optimization_barrier(jnp.sum(contracted[0] * hat_y[:, None, :], axis=0))
    along_y = lax.optimization_barrier(jnp.sum(contracted[0] * slope_y[:, None, :], axis=0))
    along_x = lax.optimization_barrier(jnp.sum(contracted[1] * hat_y[:, None, :], axis=0))
    level_value = lax.optimization_barrier(jnp.sum(value_rows * hat_z, axis=0))
    gradient = jnp.stack([lax.optimization_barrier(jnp.sum(along_x * hat_z, axis=0)), lax.optimization_barrier(jnp.sum(along_y * hat_z, axis=0)), lax.optimization_barrier(jnp.sum(value_rows * slope_z, axis=0))])
    intersection = jnp.maximum(-level_value, 0.0)
    magnitude = jnp.sqrt(lax.optimization_barrier(jnp.sum(gradient * gradient, axis=0)))
    push_scale = stiffness * intersection / jnp.maximum(magnitude, 1.0)
    force_world = jnp.dot(turn_j, gradient * push_scale[None, :], precision=highest)
    net_force = lax.optimization_barrier(jnp.sum(force_world, axis=1))
    twist_node = lax.optimization_barrier(jnp.sum(jnp.cross(node_arms, force_world, axis=0), axis=1))
    twist_grid = -lax.optimization_barrier(jnp.sum(jnp.cross(relative, force_world, axis=0), axis=1))
    return jnp.concatenate([net_force, twist_node, twist_grid])

def advance(position, quaternion, velocity, spin, mass, grain_loads):
    inertia = 0.4 * mass * (3.0 * GRID / 16.0) ** 2
    new_velocity = velocity + time_step * grain_loads[:3] / mass[None, :]
    new_spin = spin + time_step * grain_loads[3:] / inertia[None, :]
    new_position = position + time_step * new_velocity
    turning_scalar = -lax.optimization_barrier(jnp.sum(new_spin * quaternion[1:], axis=0))
    turning_vector = quaternion[0][None, :] * new_spin + jnp.cross(new_spin, quaternion[1:], axis=0)
    unnormal = quaternion + 0.5 * time_step * jnp.concatenate([turning_scalar[None, :], turning_vector])
    new_quaternion = unnormal / jnp.sqrt(lax.optimization_barrier(jnp.sum(unnormal * unnormal, axis=0)))[None, :]
    return (new_position, new_quaternion, new_velocity, new_spin)

def reference(level_set, node_coords, position, quaternion, velocity, spin, mass, grid_slot, brick_anchor, node_slot, grid_cross, anchor_cross, node_cross):
    rotations = rotation(quaternion)
    arms_all = jnp.einsum('klg,lgn->gkn', rotations, node_coords, precision=highest)
    shape_intra = (N_GROUP, N_DEV, N_DEV, SLOT_CAP)
    group_ids = jnp.arange(N_GROUP, dtype=jnp.int32).reshape(N_GROUP, 1, 1, 1)
    grid_devs = jnp.arange(N_DEV, dtype=jnp.int32).reshape(1, N_DEV, 1, 1)
    node_devs = jnp.arange(N_DEV, dtype=jnp.int32).reshape(1, 1, N_DEV, 1)
    grid_local = grid_slot.reshape(shape_intra)
    node_local = jnp.transpose(node_slot.reshape(shape_intra), (0, 2, 1, 3))
    grain_grid = (group_ids * N_DEV + grid_devs) * GRAINS_DEV + grid_local
    grain_node = (group_ids * N_DEV + node_devs) * GRAINS_DEV + jnp.maximum(node_local, 0)
    corner = jnp.moveaxis(brick_anchor.reshape((3,) + shape_intra), 0, -1)
    shape_cross = (N_GROUP, N_DEV, CROSS_CAP)
    cross_groups = jnp.arange(N_GROUP, dtype=jnp.int32).reshape(N_GROUP, 1, 1)
    cross_devs = jnp.arange(N_DEV, dtype=jnp.int32).reshape(1, N_DEV, 1)
    above_local = jnp.concatenate([node_cross.reshape(shape_cross)[1:], jnp.full((1, N_DEV, CROSS_CAP), -1, dtype=jnp.int32)], axis=0)
    cross_grid = (cross_groups * N_DEV + cross_devs) * GRAINS_DEV + grid_cross.reshape(shape_cross)
    cross_node = jnp.minimum(((cross_groups + 1) * N_DEV + cross_devs) * GRAINS_DEV + jnp.maximum(above_local, 0), GRAINS - 1)
    cross_corner = jnp.moveaxis(anchor_cross.reshape((3,) + shape_cross), 0, -1)
    pair_grid = jnp.concatenate([grain_grid.reshape(OWNERS, SLOTS), cross_grid.reshape(OWNERS, CROSS_CAP)], axis=1)
    pair_node = jnp.concatenate([grain_node.reshape(OWNERS, SLOTS), cross_node.reshape(OWNERS, CROSS_CAP)], axis=1)
    pair_valid = jnp.concatenate([(node_local >= 0).reshape(OWNERS, SLOTS), (above_local >= 0).reshape(OWNERS, CROSS_CAP)], axis=1).astype(jnp.float32)
    pair_corner = jnp.concatenate([corner.reshape(OWNERS, SLOTS, 3), cross_corner.reshape(OWNERS, CROSS_CAP, 3)], axis=1)

    def single_pair(grid_grain, node_grain, brick_corner):
        brick_vals = lax.dynamic_slice(level_set, (grid_grain, brick_corner[0], brick_corner[1], brick_corner[2]), (1, BRICK, BRICK, BRICK))[0]
        return contact(arms_all[node_grain], position[:, node_grain], brick_vals, brick_corner.astype(jnp.float32), position[:, grid_grain], rotations[:, :, grid_grain])

    def owner_pairs(pair_data):
        return jax.vmap(single_pair)(pair_data[0], pair_data[1], pair_data[2]) * pair_data[3][:, None]
    pair_loads = lax.map(owner_pairs, (pair_grid, pair_node, pair_corner, pair_valid)).reshape(-1, 9)
    load_node = pair_loads[:, :6]
    load_grid = jnp.concatenate([-pair_loads[:, :3], pair_loads[:, 6:]], axis=1)
    grain_loads = jax.ops.segment_sum(load_node, pair_node.reshape(-1), num_segments=GRAINS) + jax.ops.segment_sum(load_grid, pair_grid.reshape(-1), num_segments=GRAINS)
    new_position, new_quaternion, new_velocity, new_spin = advance(position, quaternion, velocity, spin, mass, grain_loads.T)
    return (new_position, new_quaternion, new_velocity, new_spin)
```

```python
import jax
import jax.numpy as jnp
import numpy as np
from jax import lax
from jax.experimental import pallas as pl
from jax.experimental.pallas import tpu as pltpu
from jax.sharding import PartitionSpec as P

MESH = pl.DeviceIdType.MESH
f32, bf16, i32 = jnp.float32, jnp.bfloat16, jnp.int32

GRID = 64
GROUPS = 8
DEVS = 64
GRAINS = 4
NODES = 512
BASE = GRID // 2 - 5
SPAN = 10
TILES = DEVS + 8
PAIRS = 2 * TILES
LEVELS = 32766.0
stiffness = 0.1
time_step = 0.5
R_PART = (0, 0, 1, 1, 0, 2)
P_PART = (0, 1, 0, 1, 2, 0)


def spread_matrix():
    spread = np.zeros((3 * 128, 3 * 128), np.float32)
    for k in range(3):
        for combo, part in enumerate(R_PART):
            for m in range(3):
                for grain in range(GRAINS):
                    spread[128 * part + 3 * m + k, 128 * k + 16 * combo + 4 * m + grain] = 1.0
            spread[128 * part + 9 + k, 128 * k + 16 * combo + 12] = 1.0
    return spread


def iota(shape, dim):
    return lax.broadcasted_iota(i32, shape, dim)


def parts(x):
    first = x.astype(bf16)
    rest = x - first.astype(f32)
    second = rest.astype(bf16)
    third = (rest - second.astype(f32)).astype(bf16)
    return first, second, third


def matmul(a, b):
    return jnp.dot(a, b, preferred_element_type=f32)


def matmul_nt(a, b):
    return lax.dot_general(a, b, (((1,), (1,)), ((), ())), preferred_element_type=f32)


def hat(t):
    return jnp.maximum(1.0 - jnp.abs(t), 0.0)


def slope(t):
    return jnp.maximum(jnp.minimum(-2.0 * t, jnp.maximum(t + 1.5, 0.0)), jnp.minimum(t - 1.5, 0.0))


def take(table, index):
    return jnp.take_along_axis(table, index, axis=1, mode="promise_in_bounds")


def near(u):
    r = jnp.floor(u + 0.5)
    f = u - r
    e = jnp.abs(f)
    up = f >= 0.0
    half = jnp.where(up, 0.5, -0.5)
    step = jnp.where(up, 1, -1)
    a = r.astype(i32)
    b = a + step
    c = a - step
    in_a, in_b, in_c = ((i & -8) == 0 for i in (a, b, c))
    hats = (jnp.where(in_a, 1.0 - e, 0.0), jnp.where(in_b, e, 0.0))
    slopes = (
        jnp.where(in_a, -2.0 * f, 0.0),
        jnp.where(in_b, f + half, 0.0),
        jnp.where(in_c, f - half, 0.0),
    )
    return (a & 7, b & 7, c & 7), hats, slopes


def contact(even, odd, scale, u):
    rx = jnp.floor(u[0] + 0.5).astype(i32)
    bit_e = ((rx + 1) << 4) & 64
    bit_o = ((rx - 1) << 4) & 64
    de = u[0] - (bit_e >> 4).astype(f32)
    do = u[0] - (bit_o >> 4).astype(f32) - 2.0
    tiny = 1.0 / 65536.0

    def lanes(weight):
        hi_e, hi_o = weight(de - 1.0) * tiny, weight(do - 1.0) * tiny
        return weight(de) - hi_e, hi_e, weight(do) - hi_o, hi_o

    hx, sx = lanes(hat), lanes(slope)
    yi, hy, sy = near(u[1])
    zi, hz, sz = near(u[2])
    yi = [i << 3 for i in yi]

    def column(j, k, with_slope):
        place = yi[j] | zi[k]
        we, wo = take(even, bit_e | place), take(odd, bit_o | place)
        values = (((we << 16) >> 16).astype(f32), we.astype(f32), ((wo << 16) >> 16).astype(f32), wo.astype(f32))

        def meet(w):
            return (values[0] * w[0] + values[1] * w[1]) + (values[2] * w[2] + values[3] * w[3])

        return meet(hx), (meet(sx) if with_slope else None)

    rows, rows_x, rows_z = [], [], []
    for j in range(2):
        v0, s0 = column(j, 0, True)
        v1, s1 = column(j, 1, True)
        v2, _ = column(j, 2, False)
        rows.append(v0 * hz[0] + v1 * hz[1])
        rows_x.append(s0 * hz[0] + s1 * hz[1])
        rows_z.append(v0 * sz[0] + v1 * sz[1] + v2 * sz[2])
    v0, _ = column(2, 0, False)
    v1, _ = column(2, 1, False)
    rows.append(v0 * hz[0] + v1 * hz[1])
    phi = (rows[0] * hy[0] + rows[1] * hy[1]) * scale
    gx = (rows_x[0] * hy[0] + rows_x[1] * hy[1]) * scale
    gy = (rows[0] * sy[0] + rows[1] * sy[1] + rows[2] * sy[2]) * scale
    gz = (rows_z[0] * hy[0] + rows_z[1] * hy[1]) * scale
    push = stiffness * jnp.maximum(-phi, 0.0) * lax.rsqrt(jnp.maximum(gx * gx + gy * gy + gz * gz, 1.0))
    g = (gx * push, gy * push, gz * push)
    return g + cross(u, g)


def cross(a, b):
    return (a[1] * b[2] - a[2] * b[1], a[2] * b[0] - a[0] * b[2], a[0] * b[1] - a[1] * b[0])


def kernel(
    level_ref, coords_ref, position_ref, quaternion_ref, velocity_ref, spin_ref, mass_ref, grid_ref, anchor_ref, node_ref,
    grid_cross_ref, anchor_cross_ref, node_cross_ref, spread_ref,
    new_position_ref, new_quaternion_ref, new_velocity_ref, new_spin_ref,
    window, attr, cols, slab, pose, points, out_msg, in_msg, metas, sums, out_ret, in_ret, back,
    window_sem, send_sem, recv_sem, ret_send_sem, ret_recv_sem, cross_sem,
):
    g = lax.axis_index("group")
    d = lax.axis_index("dev")
    up, down = lax.rem(g + 1, GROUPS), lax.rem(g + GROUPS - 1, GROUPS)
    barrier = pltpu.get_barrier_semaphore()

    def greet(k, _):
        e = lax.rem(d + k, DEVS)
        pl.semaphore_signal(barrier, inc=1, device_id=(g, e), device_id_type=MESH)
        return 0

    load = pltpu.make_async_copy(
        level_ref.at[:, BASE : BASE + SPAN, 16:48, :], window, window_sem
    )
    load.start()
    lax.fori_loop(1, DEVS, greet, 0)
    for other in (up, down):
        pl.semaphore_signal(barrier, inc=1, device_id=(other, d), device_id_type=MESH)

    attr[...] = jnp.zeros_like(attr)
    attr[0:1, 0:128] = (grid_ref[...] + 1).astype(f32)
    attr[0:1, 128:144] = (grid_cross_ref[...] + 1).astype(f32)
    attr[1:4, 0:128] = (anchor_ref[...] - BASE).astype(f32)
    attr[1:4, 128:144] = (anchor_cross_ref[...] - BASE).astype(f32)
    attr[4:5, 0:128] = (node_ref[...] + 1).astype(f32)
    attr[4:5, 128:144] = (node_cross_ref[...] + 1).astype(f32)
    slot_to = iota((256, 256), 0)
    order = (iota((256, 256), 1) == ((slot_to & 127) << 1) + (slot_to >> 7)).astype(f32).astype(bf16)
    attr_b = attr[...].astype(bf16)
    attr_rows = matmul_nt(attr_b, order)
    cols[...] = matmul_nt(order, attr_b)

    w, x, y, z = (quaternion_ref[k : k + 1, :] for k in range(4))
    rot = (
        1.0 - 2.0 * (y * y + z * z), 2.0 * (x * y - w * z), 2.0 * (x * z + w * y),
        2.0 * (x * y + w * z), 1.0 - 2.0 * (x * x + z * z), 2.0 * (y * z - w * x),
        2.0 * (x * z - w * y), 2.0 * (y * z + w * x), 1.0 - 2.0 * (x * x + y * y),
    )
    pos = [position_ref[m : m + 1, :] for m in range(3)]
    pose[...] = jnp.zeros_like(pose)
    for n in range(9):
        pose[n : n + 1, 0:GRAINS] = rot[n]
    for k in range(3):
        turned = rot[k] * pos[0] + rot[3 + k] * pos[1] + rot[6 + k] * pos[2]
        pose[9 + k : 10 + k, 0:GRAINS] = ((GRID - 1) / 2.0 - BASE) - turned
        pose[16 + k : 17 + k, 0:GRAINS] = pos[k]
    pose_cols = pose[...].T

    points[...] = jnp.zeros_like(points)
    world = []
    for m in range(3):
        p = pose_cols[0:GRAINS, 16 + m : 17 + m]
        for n in range(3):
            p = p + pose_cols[0:GRAINS, 3 * m + n : 3 * m + n + 1] * coords_ref[n]
        world.append(p)
    ones = jnp.where(iota((GRAINS, NODES), 0) == 0, 1.0, 0.0)
    world = parts(jnp.concatenate(world + [ones], axis=0))
    for combo, part in enumerate(P_PART):
        points[16 * combo : 16 * combo + 16, :] = world[part]

    lane64 = iota((64, 384), 1)
    select_z = (iota((64, 384), 0) == BASE + (lane64 >> 7) + (lane64 & 7)).astype(f32).astype(bf16)
    place_y = iota((16, 128), 0)
    lane_y = (iota((16, 128), 1) >> 3) & 7
    load.wait()
    planes = matmul(window[...].reshape(GRAINS * SPAN * 32, GRID), select_z)
    planes = planes.reshape(GRAINS * SPAN, 32, 384)[:, 8:24, :]
    low_half = iota((40, 128), 1) < 64
    for ay in range(3):
        keep = (place_y == BASE - 24 + ay + lane_y).astype(f32)
        for az in range(3):
            picked = jnp.sum(planes[:, :, 128 * az : 128 * az + 128] * keep[None], axis=1)
            q = 3 * ay + az
            slab[40 * q : 40 * q + 40, :] = jnp.where(low_half, picked, pltpu.roll(picked, 36, 0))
    slab[360:384, :] = jnp.zeros((24, 128), f32)
    code = [
        (cols[128 * c : 128 * c + TILES, 2:3] * 3.0 + cols[128 * c : 128 * c + TILES, 3:4]) * 40.0
        + (cols[128 * c : 128 * c + TILES, 0:1] - 1.0) * 10.0
        + cols[128 * c : 128 * c + TILES, 1:2]
        for c in range(2)
    ]
    code = jnp.concatenate([code[c] + float(j) for c in range(2) for j in range(4)], axis=0).astype(i32)
    pick = (iota((8 * TILES, 384), 1) == code).astype(f32).astype(bf16)
    bricks = matmul(pick, slab[...].astype(bf16))
    lane = iota((TILES, 128), 1)
    pose_parts = parts(pose_cols)
    unit = jnp.where(lane < 9, 2.0**30, jnp.where(lane < 12, 2.0**27, 2.0**28))
    for c in range(2):
        rows = [bricks[TILES * (4 * c + j) : TILES * (4 * c + j + 1), :] for j in range(4)]
        most = jnp.maximum(
            jnp.maximum(jnp.abs(rows[0]), jnp.abs(rows[1])), jnp.maximum(jnp.abs(rows[2]), jnp.abs(rows[3]))
        )
        most = jnp.maximum(jnp.max(most, axis=1, keepdims=True), 1e-6)
        inverse = LEVELS / most
        level = [jnp.floor(row * inverse + 0.5).astype(i32) for row in rows]
        out_msg[pl.ds(3 * c, TILES, stride=8), :] = (level[1] << 16) + level[0]
        out_msg[pl.ds(3 * c + 1, TILES, stride=8), :] = (level[3] << 16) + level[2]
        own = cols[128 * c : 128 * c + TILES, :]
        grain = (own[:, 0:1].astype(i32) - 1 == lane).astype(f32).astype(bf16)
        meta = matmul(grain, pose_parts[0]) + matmul(grain, pose_parts[1]) + matmul(grain, pose_parts[2])
        for k in range(3):
            meta = meta - jnp.where(lane == 9 + k, own[:, 1 + k : 2 + k], 0.0)
        meta = jnp.where(lane == 12, most, jnp.where(lane < 12, meta, 0.0))
        out_msg[pl.ds(3 * c + 2, TILES, stride=8), :] = (meta * unit).astype(i32)

    def message(e, other):
        return pltpu.make_async_remote_copy(
            src_ref=out_msg.at[pl.ds(pl.multiple_of(8 * e, 8), ROWS)],
            dst_ref=in_msg.at[pl.ds(pl.multiple_of(8 * other, 8), ROWS)],
            send_sem=send_sem.at[e],
            recv_sem=recv_sem.at[other],
            device_id=(g, e),
            device_id_type=MESH,
        )

    def reply(e, other):
        return pltpu.make_async_remote_copy(
            src_ref=out_ret.at[e],
            dst_ref=in_ret.at[other],
            send_sem=ret_send_sem.at[e],
            recv_sem=ret_recv_sem.at[other],
            device_id=(g, e),
            device_id_type=MESH,
        )

    cross_message = pltpu.make_async_remote_copy(
        src_ref=out_msg.at[pl.ds(8 * DEVS, 64)],
        dst_ref=in_msg.at[pl.ds(8 * DEVS, 64)],
        send_sem=cross_sem.at[0],
        recv_sem=cross_sem.at[1],
        device_id=(up, d),
        device_id_type=MESH,
    )
    cross_reply = pltpu.make_async_remote_copy(
        src_ref=out_ret.at[pl.ds(DEVS, 8)],
        dst_ref=in_ret.at[pl.ds(DEVS, 8)],
        send_sem=cross_sem.at[2],
        recv_sem=cross_sem.at[3],
        device_id=(down, d),
        device_id_type=MESH,
    )
    own_message = pltpu.make_async_copy(
        out_msg.at[pl.ds(pl.multiple_of(8 * d, 8), ROWS)], in_msg.at[pl.ds(pl.multiple_of(8 * d, 8), ROWS)], recv_sem.at[d]
    )
    own_reply = pltpu.make_async_copy(out_ret.at[d], in_ret.at[d], ret_recv_sem.at[d])

    def octet(t):
        far = (t + 1) // 2
        shift = jnp.where(t % 2 == 1, far, 8 - far)
        return (d // 8 + shift) % 8

    pl.semaphore_wait(barrier, DEVS + 1)
    own_message.start()

    def send_octet(t, _):
        base = 8 * octet(t)

        def send(i, _):
            e = base + (d + i) % 8

            @pl.when(e != d)
            def _():
                message(e, d).start()

            return 0

        lax.fori_loop(0, 8, send, 0)
        return 0

    cross_message.start()
    lax.fori_loop(0, 8, send_octet, 0)

    metas[...] = jnp.zeros_like(metas)
    sums[...] = jnp.zeros_like(sums)
    back[...] = jnp.zeros_like(back)
    lane8 = iota((8, 128), 1)
    lane16 = iota((16, 128), 1)
    per_lane = jnp.where(lane8 < 9, 2.0**-30, jnp.where(lane8 < 12, 2.0**-27, 2.0**-28 / LEVELS))

    def work(t, _):
        is_cross = t == 1
        vg = jnp.where(is_cross, 8, octet(jnp.where(t > 1, t - 1, 0)))

        @pl.when(is_cross)
        def _():
            cross_message.wait_recv()

        @pl.when(t != 1)
        def _():
            def await_one(i, _):
                message(8 * vg + i, 8 * vg + i).wait_recv()
                return 0

            lax.fori_loop(0, 8, await_one, 0)

        at = pl.multiple_of(64 * vg, 64)
        meta = []
        node = []
        for c in range(2):
            row = in_msg[pl.ds(at + 3 * c + 2, 8, stride=8), :].astype(f32) * per_lane
            metas[pl.ds(pl.multiple_of(128 * c + 8 * vg, 8), 8), :] = row
            meta.append(row)
            node.append(cols[pl.ds(pl.multiple_of(128 * c + 8 * vg, 8), 8), :][:, 4:5])
        spread = matmul(jnp.concatenate(parts(jnp.concatenate(meta, axis=0)), axis=1), spread_ref[...])
        mine = (lane16 & 3) == jnp.concatenate(node, axis=0).astype(i32) - 1
        mine = jnp.logical_or(mine, (lane16 & 15) == 12)
        left = jnp.concatenate(
            [jnp.where(mine, spread[:, 128 * k : 128 * k + 128], 0.0) for k in range(3)], axis=0
        ).astype(bf16)
        place = matmul(left, points[...])
        result = jnp.zeros((8, 128), f32)
        for c in range(2):
            even = in_msg[pl.ds(at + 3 * c, 8, stride=8), :]
            odd = in_msg[pl.ds(at + 3 * c + 1, 8, stride=8), :]
            scale = jnp.broadcast_to(jnp.where(node[c] > 0.5, meta[c][:, 12:13], 0.0), (8, 128))
            total = None
            for chunk in range(NODES // 128):
                u = tuple(place[16 * k + 8 * c : 16 * k + 8 * c + 8, 128 * chunk : 128 * chunk + 128] for k in range(3))
                term = contact(even, odd, scale, u)
                total = term if total is None else tuple(a + b for a, b in zip(total, term))
            for n in range(6):
                result = jnp.where(lane8 == 8 * c + n, jnp.sum(total[n], axis=1, keepdims=True), result)
        sums[pl.ds(pl.multiple_of(8 * vg, 8), 8), :] = result
        out_ret[pl.ds(8 * vg, 8), 0, :] = result

        @pl.when(is_cross)
        def _():
            cross_reply.start()

        @pl.when(t != 1)
        def _():
            def answer(i, _):
                e = 8 * vg + i

                @pl.when(e != d)
                def _():
                    reply(e, d).start()

                @pl.when(e == d)
                def _():
                    own_reply.start()

                return 0

            lax.fori_loop(0, 8, answer, 0)

        return 0

    lax.fori_loop(0, 9, work, 0)

    sums_t = sums[...].T
    lane_p = iota((8, 128), 1)
    row_p = iota((8, 128), 0)

    def per_grain(tables, masks):
        out = jnp.zeros((8, 128), f32)
        for grain in range(GRAINS):
            kept = sum(jnp.where(masks[c] == grain + 1.0, tables[c], 0.0) for c in range(2))
            out = jnp.where(lane_p == grain, jnp.sum(kept, axis=1, keepdims=True), out)
        return out

    def stack(rows):
        out = jnp.zeros((8, 128), f32)
        for n, row in enumerate(rows):
            out = jnp.where(row_p == n, row, out)
        return out

    node_tables, node_masks = [], []
    for c in range(2):
        meta_t = metas[128 * c : 128 * c + 128, :].T
        r = [[meta_t[3 * m + k : 3 * m + k + 1, :] for k in range(3)] for m in range(3)]
        mask = attr_rows[4:5, 128 * c : 128 * c + 128]
        centre = []
        for m in range(3):
            value = jnp.zeros((1, 128), f32)
            for grain in range(GRAINS):
                value = jnp.where(mask == grain + 1.0, pose[16 + m : 17 + m, grain : grain + 1], value)
            centre.append(value)
        shift = [r[0][k] * centre[0] + r[1][k] * centre[1] + r[2][k] * centre[2] + meta_t[9 + k : 10 + k, :] for k in range(3)]
        push = [sums_t[8 * c + n : 8 * c + n + 1, :] for n in range(3)]
        twist = [sums_t[8 * c + 3 + n : 8 * c + 4 + n, :] for n in range(3)]
        lever = cross(shift, push)
        twist = [twist[n] - lever[n] for n in range(3)]
        rows = [r[m][0] * v[0] + r[m][1] * v[1] + r[m][2] * v[2] for v in (push, twist) for m in range(3)]
        node_tables.append(stack(rows))
        node_masks.append(mask)
    node_load = per_grain(node_tables, node_masks)

    def await_reply(e, _):
        reply(e, e).wait_recv()
        return 0

    lax.fori_loop(0, DEVS, await_reply, 0)
    cross_reply.wait_recv()
    back[0:TILES, :] = in_ret[:, 0, :]
    back_t = back[...].T
    grid_tables, grid_masks = [], []
    for c in range(2):
        corner = [((GRID - 1) / 2.0 - BASE) - attr_rows[1 + k : 2 + k, 128 * c : 128 * c + 128] for k in range(3)]
        push = [back_t[8 * c + n : 8 * c + n + 1, :] for n in range(3)]
        lever = cross(corner, push)
        twist = [back_t[8 * c + 3 + n : 8 * c + 4 + n, :] - lever[n] for n in range(3)]
        grid_tables.append(stack(push + twist))
        grid_masks.append(attr_rows[0:1, 128 * c : 128 * c + 128])
    grid_load = per_grain(grid_tables, grid_masks)

    def turn(first):
        v = [grid_load[first + k : first + k + 1, 0:GRAINS] for k in range(3)]
        return [rot[3 * m] * v[0] + rot[3 * m + 1] * v[1] + rot[3 * m + 2] * v[2] for m in range(3)]

    force, torque = turn(0), turn(3)
    force = [node_load[m : m + 1, 0:GRAINS] - force[m] for m in range(3)]
    torque = [node_load[3 + m : 4 + m, 0:GRAINS] - torque[m] for m in range(3)]
    mass = mass_ref[...]
    gain = time_step / mass
    spin_gain = time_step / (0.4 * mass * (3.0 * GRID / 16.0) ** 2)
    vel = [velocity_ref[m : m + 1, :] + force[m] * gain for m in range(3)]
    spin = [spin_ref[m : m + 1, :] + torque[m] * spin_gain for m in range(3)]
    for m in range(3):
        new_velocity_ref[m : m + 1, :] = vel[m]
        new_spin_ref[m : m + 1, :] = spin[m]
        new_position_ref[m : m + 1, :] = pos[m] + time_step * vel[m]
    vec = (x, y, z)
    turned = cross(spin, vec)
    quarter = 0.5 * time_step
    q = [w - quarter * (spin[0] * x + spin[1] * y + spin[2] * z)]
    q += [vec[m] + quarter * (w * spin[m] + turned[m]) for m in range(3)]
    norm = jnp.sqrt(q[0] * q[0] + q[1] * q[1] + q[2] * q[2] + q[3] * q[3])
    for k in range(4):
        new_quaternion_ref[k : k + 1, :] = q[k] / norm

    def finish(e, _):
        @pl.when(e != d)
        def _():
            message(e, d).wait_send()
            reply(e, d).wait_send()

        return 0

    lax.fori_loop(0, DEVS, finish, 0)
    cross_message.wait_send()
    cross_reply.wait_send()


ROWS = 6


def body(
    level_set, node_coords, position, quaternion, velocity, spin, mass, grid_slot, brick_anchor, node_slot, grid_cross,
    anchor_cross, node_cross,
):
    vmem = pl.BlockSpec(memory_space=pltpu.VMEM)
    dma = pltpu.SemaphoreType.DMA
    row = lambda a: a.reshape(1, -1)
    outs = pl.pallas_call(
        kernel,
        out_shape=[jax.ShapeDtypeStruct((n, GRAINS), f32) for n in (3, 4, 3, 3)],
        in_specs=[pl.BlockSpec(memory_space=pl.ANY)] + [vmem] * 13,
        out_specs=[vmem] * 4,
        scratch_shapes=[
            pltpu.VMEM((GRAINS, SPAN, 32, GRID), bf16),
            pltpu.VMEM((128, 256), f32),
            pltpu.VMEM((256, 128), f32),
            pltpu.VMEM((384, 128), f32),
            pltpu.VMEM((128, 128), f32),
            pltpu.VMEM((128, NODES), bf16),
            pltpu.VMEM((8 * TILES, 128), i32),
            pltpu.VMEM((8 * TILES, 128), i32),
            pltpu.VMEM((256, 128), f32),
            pltpu.VMEM((128, 128), f32),
            pltpu.VMEM((TILES, 1, 128), f32),
            pltpu.VMEM((TILES, 1, 128), f32),
            pltpu.VMEM((128, 128), f32),
            dma,
            dma((DEVS,)),
            dma((DEVS,)),
            dma((DEVS,)),
            dma((DEVS,)),
            dma((4,)),
        ],
        compiler_params=pltpu.CompilerParams(
            collective_id=0, has_side_effects=True, vmem_limit_bytes=32 * 1024 * 1024
        ),
    )(
        level_set, node_coords, position, quaternion, velocity, spin, row(mass), row(grid_slot), brick_anchor, row(node_slot),
        row(grid_cross), anchor_cross, row(node_cross), jnp.asarray(spread_matrix(), bf16),
    )
    return tuple(outs)


def solution(mesh):
    both = ("group", "dev")
    wide, flat = P(None, both), P(both)
    in_specs = (
        P(both, None, None, None), P(None, both, None), wide, wide, wide, wide, flat, flat, wide, flat, flat, wide, flat,
    )
    return jax.shard_map(body, mesh=mesh, in_specs=in_specs, out_specs=(wide,) * 4, check_vma=False)
```

```python
import jax
import jax.numpy as jnp
import numpy as np
from jax import lax
from jax.experimental import pallas as pl
from jax.experimental.pallas import tpu as pltpu
from jax.sharding import PartitionSpec as P

MESH = pl.DeviceIdType.MESH
f32, bf16, i32 = jnp.float32, jnp.bfloat16, jnp.int32

GRID = 64
GROUPS = 8
DEVS = 64
GRAINS = 4
NODES = 512
BASE = GRID // 2 - 5
SPAN = 10
TILES = DEVS + 8
PAIRS = 2 * TILES
LEVELS = 32766.0
stiffness = 0.1
time_step = 0.5
R_PART = (0, 0, 1, 1, 0, 2)
P_PART = (0, 1, 0, 1, 2, 0)


def spread_matrix():
    spread = np.zeros((3 * 128, 3 * 128), np.float32)
    for k in range(3):
        for combo, part in enumerate(R_PART):
            for m in range(3):
                for grain in range(GRAINS):
                    spread[128 * part + 3 * m + k, 128 * k + 16 * combo + 4 * m + grain] = 1.0
            spread[128 * part + 9 + k, 128 * k + 16 * combo + 12] = 1.0
    return spread


def iota(shape, dim):
    return lax.broadcasted_iota(i32, shape, dim)


def parts(x):
    first = x.astype(bf16)
    rest = x - first.astype(f32)
    second = rest.astype(bf16)
    third = (rest - second.astype(f32)).astype(bf16)
    return first, second, third


def matmul(a, b):
    return jnp.dot(a, b, preferred_element_type=f32)


def matmul_nt(a, b):
    return lax.dot_general(a, b, (((1,), (1,)), ((), ())), preferred_element_type=f32)


def hat(t):
    return jnp.maximum(1.0 - jnp.abs(t), 0.0)


def slope(t):
    return jnp.maximum(jnp.minimum(-2.0 * t, jnp.maximum(t + 1.5, 0.0)), jnp.minimum(t - 1.5, 0.0))


def take(table, index):
    return jnp.take_along_axis(table, index, axis=1, mode="promise_in_bounds")


def near(u):
    r = jnp.floor(u + 0.5)
    f = u - r
    e = jnp.abs(f)
    up = f >= 0.0
    half = jnp.where(up, 0.5, -0.5)
    step = jnp.where(up, 1, -1)
    a = r.astype(i32)
    b = a + step
    c = a - step
    in_a, in_b, in_c = ((i & -8) == 0 for i in (a, b, c))
    hats = (jnp.where(in_a, 1.0 - e, 0.0), jnp.where(in_b, e, 0.0))
    slopes = (
        jnp.where(in_a, -2.0 * f, 0.0),
        jnp.where(in_b, f + half, 0.0),
        jnp.where(in_c, f - half, 0.0),
    )
    return (a & 7, b & 7, c & 7), hats, slopes


def contact(even, odd, scale, u):
    rx = jnp.floor(u[0] + 0.5).astype(i32)
    bit_e = ((rx + 1) << 4) & 64
    bit_o = ((rx - 1) << 4) & 64
    de = u[0] - (bit_e >> 4).astype(f32)
    do = u[0] - (bit_o >> 4).astype(f32) - 2.0
    tiny = 1.0 / 65536.0

    def lanes(weight):
        hi_e, hi_o = weight(de - 1.0) * tiny, weight(do - 1.0) * tiny
        return weight(de) - hi_e, hi_e, weight(do) - hi_o, hi_o

    hx, sx = lanes(hat), lanes(slope)
    yi, hy, sy = near(u[1])
    zi, hz, sz = near(u[2])
    yi = [i << 3 for i in yi]

    def column(j, k, with_slope):
        place = yi[j] | zi[k]
        we, wo = take(even, bit_e | place), take(odd, bit_o | place)
        values = (((we << 16) >> 16).astype(f32), we.astype(f32), ((wo << 16) >> 16).astype(f32), wo.astype(f32))

        def meet(w):
            return (values[0] * w[0] + values[1] * w[1]) + (values[2] * w[2] + values[3] * w[3])

        return meet(hx), (meet(sx) if with_slope else None)

    rows, rows_x, rows_z = [], [], []
    for j in range(2):
        v0, s0 = column(j, 0, True)
        v1, s1 = column(j, 1, True)
        v2, _ = column(j, 2, False)
        rows.append(v0 * hz[0] + v1 * hz[1])
        rows_x.append(s0 * hz[0] + s1 * hz[1])
        rows_z.append(v0 * sz[0] + v1 * sz[1] + v2 * sz[2])
    v0, _ = column(2, 0, False)
    v1, _ = column(2, 1, False)
    rows.append(v0 * hz[0] + v1 * hz[1])
    phi = (rows[0] * hy[0] + rows[1] * hy[1]) * scale
    gx = (rows_x[0] * hy[0] + rows_x[1] * hy[1]) * scale
    gy = (rows[0] * sy[0] + rows[1] * sy[1] + rows[2] * sy[2]) * scale
    gz = (rows_z[0] * hy[0] + rows_z[1] * hy[1]) * scale
    push = stiffness * jnp.maximum(-phi, 0.0) * lax.rsqrt(jnp.maximum(gx * gx + gy * gy + gz * gz, 1.0))
    g = (gx * push, gy * push, gz * push)
    return g + cross(u, g)


def cross(a, b):
    return (a[1] * b[2] - a[2] * b[1], a[2] * b[0] - a[0] * b[2], a[0] * b[1] - a[1] * b[0])


def kernel(
    level_ref, *refs
):
    sources, refs = refs[:SMALL], refs[SMALL:]
    (
        new_position_ref, new_quaternion_ref, new_velocity_ref, new_spin_ref,
        window, attr, cols, slab, pose, points, out_msg, in_msg, metas, sums, out_ret, in_ret, back,
        window_sem, send_sem, recv_sem, ret_send_sem, ret_recv_sem, cross_sem, input_sem,
    ) = refs[:SCRATCH]
    inputs = refs[SCRATCH:]
    (
        coords_ref, position_ref, quaternion_ref, velocity_ref, spin_ref, mass_ref, grid_ref, anchor_ref, node_ref,
        grid_cross_ref, anchor_cross_ref, node_cross_ref, spread_ref,
    ) = inputs
    g = lax.axis_index("group")
    d = lax.axis_index("dev")
    up, down = lax.rem(g + 1, GROUPS), lax.rem(g + GROUPS - 1, GROUPS)
    barrier = pltpu.get_barrier_semaphore()

    def greet(k, _):
        e = lax.rem(d + k, DEVS)
        pl.semaphore_signal(barrier, inc=1, device_id=(g, e), device_id_type=MESH)
        return 0

    load = pltpu.make_async_copy(
        level_ref.at[:, BASE : BASE + SPAN, 16:48, :], window, window_sem
    )
    load.start()
    fetches = [
        pltpu.make_async_copy(source, target, input_sem.at[n])
        for n, (source, target) in enumerate(zip(sources, inputs))
    ]
    for fetch in fetches:
        fetch.start()
    lax.fori_loop(1, DEVS, greet, 0)
    for other in (up, down):
        pl.semaphore_signal(barrier, inc=1, device_id=(other, d), device_id_type=MESH)

    for fetch in fetches:
        fetch.wait()

    attr[...] = jnp.zeros_like(attr)
    attr[0:1, 0:128] = (grid_ref[...] + 1).astype(f32)
    attr[0:1, 128:144] = (grid_cross_ref[...] + 1).astype(f32)
    attr[1:4, 0:128] = (anchor_ref[...] - BASE).astype(f32)
    attr[1:4, 128:144] = (anchor_cross_ref[...] - BASE).astype(f32)
    attr[4:5, 0:128] = (node_ref[...] + 1).astype(f32)
    attr[4:5, 128:144] = (node_cross_ref[...] + 1).astype(f32)
    slot_to = iota((256, 256), 0)
    order = (iota((256, 256), 1) == ((slot_to & 127) << 1) + (slot_to >> 7)).astype(f32).astype(bf16)
    attr_b = attr[...].astype(bf16)
    attr_rows = matmul_nt(attr_b, order)
    cols[...] = matmul_nt(order, attr_b)

    w, x, y, z = (quaternion_ref[k : k + 1, :] for k in range(4))
    rot = (
        1.0 - 2.0 * (y * y + z * z), 2.0 * (x * y - w * z), 2.0 * (x * z + w * y),
        2.0 * (x * y + w * z), 1.0 - 2.0 * (x * x + z * z), 2.0 * (y * z - w * x),
        2.0 * (x * z - w * y), 2.0 * (y * z + w * x), 1.0 - 2.0 * (x * x + y * y),
    )
    pos = [position_ref[m : m + 1, :] for m in range(3)]
    pose[...] = jnp.zeros_like(pose)
    for n in range(9):
        pose[n : n + 1, 0:GRAINS] = rot[n]
    for k in range(3):
        turned = rot[k] * pos[0] + rot[3 + k] * pos[1] + rot[6 + k] * pos[2]
        pose[9 + k : 10 + k, 0:GRAINS] = ((GRID - 1) / 2.0 - BASE) - turned
        pose[16 + k : 17 + k, 0:GRAINS] = pos[k]
    pose_cols = pose[...].T

    points[...] = jnp.zeros_like(points)
    world = []
    for m in range(3):
        p = pose_cols[0:GRAINS, 16 + m : 17 + m]
        for n in range(3):
            p = p + pose_cols[0:GRAINS, 3 * m + n : 3 * m + n + 1] * coords_ref[n]
        world.append(p)
    ones = jnp.where(iota((GRAINS, NODES), 0) == 0, 1.0, 0.0)
    world = parts(jnp.concatenate(world + [ones], axis=0))
    for combo, part in enumerate(P_PART):
        points[16 * combo : 16 * combo + 16, :] = world[part]

    lane64 = iota((64, 384), 1)
    select_z = (iota((64, 384), 0) == BASE + (lane64 >> 7) + (lane64 & 7)).astype(f32).astype(bf16)
    place_y = iota((16, 128), 0)
    lane_y = (iota((16, 128), 1) >> 3) & 7
    load.wait()
    planes = matmul(window[...].reshape(GRAINS * SPAN * 32, GRID), select_z)
    planes = planes.reshape(GRAINS * SPAN, 32, 384)[:, 8:24, :]
    low_half = iota((40, 128), 1) < 64
    for ay in range(3):
        keep = (place_y == BASE - 24 + ay + lane_y).astype(f32)
        for az in range(3):
            picked = jnp.sum(planes[:, :, 128 * az : 128 * az + 128] * keep[None], axis=1)
            q = 3 * ay + az
            slab[40 * q : 40 * q + 40, :] = jnp.where(low_half, picked, pltpu.roll(picked, 36, 0))
    slab[360:384, :] = jnp.zeros((24, 128), f32)
    code = [
        (cols[128 * c : 128 * c + TILES, 2:3] * 3.0 + cols[128 * c : 128 * c + TILES, 3:4]) * 40.0
        + (cols[128 * c : 128 * c + TILES, 0:1] - 1.0) * 10.0
        + cols[128 * c : 128 * c + TILES, 1:2]
        for c in range(2)
    ]
    code = jnp.concatenate([code[c] + float(j) for c in range(2) for j in range(4)], axis=0).astype(i32)
    pick = (iota((8 * TILES, 384), 1) == code).astype(f32).astype(bf16)
    bricks = matmul(pick, slab[...].astype(bf16))
    lane = iota((TILES, 128), 1)
    pose_parts = parts(pose_cols)
    unit = jnp.where(lane < 9, 2.0**30, jnp.where(lane < 12, 2.0**27, 2.0**28))
    for c in range(2):
        rows = [bricks[TILES * (4 * c + j) : TILES * (4 * c + j + 1), :] for j in range(4)]
        most = jnp.maximum(
            jnp.maximum(jnp.abs(rows[0]), jnp.abs(rows[1])), jnp.maximum(jnp.abs(rows[2]), jnp.abs(rows[3]))
        )
        most = jnp.maximum(jnp.max(most, axis=1, keepdims=True), 1e-6)
        inverse = LEVELS / most
        level = [jnp.floor(row * inverse + 0.5).astype(i32) for row in rows]
        out_msg[pl.ds(3 * c, TILES, stride=8), :] = (level[1] << 16) + level[0]
        out_msg[pl.ds(3 * c + 1, TILES, stride=8), :] = (level[3] << 16) + level[2]
        own = cols[128 * c : 128 * c + TILES, :]
        grain = (own[:, 0:1].astype(i32) - 1 == lane).astype(f32).astype(bf16)
        meta = matmul(grain, pose_parts[0]) + matmul(grain, pose_parts[1]) + matmul(grain, pose_parts[2])
        for k in range(3):
            meta = meta - jnp.where(lane == 9 + k, own[:, 1 + k : 2 + k], 0.0)
        meta = jnp.where(lane == 12, most, jnp.where(lane < 12, meta, 0.0))
        out_msg[pl.ds(3 * c + 2, TILES, stride=8), :] = (meta * unit).astype(i32)

    def message(e, other):
        return pltpu.make_async_remote_copy(
            src_ref=out_msg.at[pl.ds(pl.multiple_of(8 * e, 8), ROWS)],
            dst_ref=in_msg.at[pl.ds(pl.multiple_of(8 * other, 8), ROWS)],
            send_sem=send_sem.at[e],
            recv_sem=recv_sem.at[other],
            device_id=(g, e),
            device_id_type=MESH,
        )

    def reply(e, other):
        return pltpu.make_async_remote_copy(
            src_ref=out_ret.at[e],
            dst_ref=in_ret.at[other],
            send_sem=ret_send_sem.at[e],
            recv_sem=ret_recv_sem.at[other],
            device_id=(g, e),
            device_id_type=MESH,
        )

    cross_message = pltpu.make_async_remote_copy(
        src_ref=out_msg.at[pl.ds(8 * DEVS, 64)],
        dst_ref=in_msg.at[pl.ds(8 * DEVS, 64)],
        send_sem=cross_sem.at[0],
        recv_sem=cross_sem.at[1],
        device_id=(up, d),
        device_id_type=MESH,
    )
    cross_reply = pltpu.make_async_remote_copy(
        src_ref=out_ret.at[pl.ds(DEVS, 8)],
        dst_ref=in_ret.at[pl.ds(DEVS, 8)],
        send_sem=cross_sem.at[2],
        recv_sem=cross_sem.at[3],
        device_id=(down, d),
        device_id_type=MESH,
    )
    own_message = pltpu.make_async_copy(
        out_msg.at[pl.ds(pl.multiple_of(8 * d, 8), ROWS)], in_msg.at[pl.ds(pl.multiple_of(8 * d, 8), ROWS)], recv_sem.at[d]
    )
    own_reply = pltpu.make_async_copy(out_ret.at[d], in_ret.at[d], ret_recv_sem.at[d])

    def octet(t):
        far = (t + 1) // 2
        shift = jnp.where(t % 2 == 1, far, 8 - far)
        return (d // 8 + shift) % 8

    pl.semaphore_wait(barrier, DEVS + 1)
    own_message.start()

    def send_octet(t, _):
        base = 8 * octet(t)

        def send(i, _):
            e = base + (d + i) % 8

            @pl.when(e != d)
            def _():
                message(e, d).start()

            return 0

        lax.fori_loop(0, 8, send, 0)
        return 0

    cross_message.start()
    lax.fori_loop(0, 8, send_octet, 0)

    metas[...] = jnp.zeros_like(metas)
    sums[...] = jnp.zeros_like(sums)
    back[...] = jnp.zeros_like(back)
    lane8 = iota((8, 128), 1)
    lane16 = iota((16, 128), 1)
    per_lane = jnp.where(lane8 < 9, 2.0**-30, jnp.where(lane8 < 12, 2.0**-27, 2.0**-28 / LEVELS))

    def work(t, _):
        is_cross = t == 1
        vg = jnp.where(is_cross, 8, octet(jnp.where(t > 1, t - 1, 0)))

        @pl.when(is_cross)
        def _():
            cross_message.wait_recv()

        @pl.when(t != 1)
        def _():
            def await_one(i, _):
                message(8 * vg + i, 8 * vg + i).wait_recv()
                return 0

            lax.fori_loop(0, 8, await_one, 0)

        at = pl.multiple_of(64 * vg, 64)
        meta = []
        node = []
        for c in range(2):
            row = in_msg[pl.ds(at + 3 * c + 2, 8, stride=8), :].astype(f32) * per_lane
            metas[pl.ds(pl.multiple_of(128 * c + 8 * vg, 8), 8), :] = row
            meta.append(row)
            node.append(cols[pl.ds(pl.multiple_of(128 * c + 8 * vg, 8), 8), :][:, 4:5])
        spread = matmul(jnp.concatenate(parts(jnp.concatenate(meta, axis=0)), axis=1), spread_ref[...])
        mine = (lane16 & 3) == jnp.concatenate(node, axis=0).astype(i32) - 1
        mine = jnp.logical_or(mine, (lane16 & 15) == 12)
        left = jnp.concatenate(
            [jnp.where(mine, spread[:, 128 * k : 128 * k + 128], 0.0) for k in range(3)], axis=0
        ).astype(bf16)
        place = matmul(left, points[...])
        result = jnp.zeros((8, 128), f32)
        for c in range(2):
            even = in_msg[pl.ds(at + 3 * c, 8, stride=8), :]
            odd = in_msg[pl.ds(at + 3 * c + 1, 8, stride=8), :]
            scale = jnp.broadcast_to(jnp.where(node[c] > 0.5, meta[c][:, 12:13], 0.0), (8, 128))
            total = None
            for chunk in range(NODES // 128):
                u = tuple(place[16 * k + 8 * c : 16 * k + 8 * c + 8, 128 * chunk : 128 * chunk + 128] for k in range(3))
                term = contact(even, odd, scale, u)
                total = term if total is None else tuple(a + b for a, b in zip(total, term))
            for n in range(6):
                result = jnp.where(lane8 == 8 * c + n, jnp.sum(total[n], axis=1, keepdims=True), result)
        sums[pl.ds(pl.multiple_of(8 * vg, 8), 8), :] = result
        out_ret[pl.ds(8 * vg, 8), 0, :] = result

        @pl.when(is_cross)
        def _():
            cross_reply.start()

        @pl.when(t != 1)
        def _():
            def answer(i, _):
                e = 8 * vg + i

                @pl.when(e != d)
                def _():
                    reply(e, d).start()

                @pl.when(e == d)
                def _():
                    own_reply.start()

                return 0

            lax.fori_loop(0, 8, answer, 0)

        return 0

    lax.fori_loop(0, 9, work, 0)

    sums_t = sums[...].T
    lane_p = iota((8, 128), 1)
    row_p = iota((8, 128), 0)

    def per_grain(tables, masks):
        out = jnp.zeros((8, 128), f32)
        for grain in range(GRAINS):
            kept = sum(jnp.where(masks[c] == grain + 1.0, tables[c], 0.0) for c in range(2))
            out = jnp.where(lane_p == grain, jnp.sum(kept, axis=1, keepdims=True), out)
        return out

    def stack(rows):
        out = jnp.zeros((8, 128), f32)
        for n, row in enumerate(rows):
            out = jnp.where(row_p == n, row, out)
        return out

    node_tables, node_masks = [], []
    for c in range(2):
        meta_t = metas[128 * c : 128 * c + 128, :].T
        r = [[meta_t[3 * m + k : 3 * m + k + 1, :] for k in range(3)] for m in range(3)]
        mask = attr_rows[4:5, 128 * c : 128 * c + 128]
        centre = []
        for m in range(3):
            value = jnp.zeros((1, 128), f32)
            for grain in range(GRAINS):
                value = jnp.where(mask == grain + 1.0, pose[16 + m : 17 + m, grain : grain + 1], value)
            centre.append(value)
        shift = [r[0][k] * centre[0] + r[1][k] * centre[1] + r[2][k] * centre[2] + meta_t[9 + k : 10 + k, :] for k in range(3)]
        push = [sums_t[8 * c + n : 8 * c + n + 1, :] for n in range(3)]
        twist = [sums_t[8 * c + 3 + n : 8 * c + 4 + n, :] for n in range(3)]
        lever = cross(shift, push)
        twist = [twist[n] - lever[n] for n in range(3)]
        rows = [r[m][0] * v[0] + r[m][1] * v[1] + r[m][2] * v[2] for v in (push, twist) for m in range(3)]
        node_tables.append(stack(rows))
        node_masks.append(mask)
    node_load = per_grain(node_tables, node_masks)

    def await_reply(e, _):
        reply(e, e).wait_recv()
        return 0

    lax.fori_loop(0, DEVS, await_reply, 0)
    cross_reply.wait_recv()
    back[0:TILES, :] = in_ret[:, 0, :]
    back_t = back[...].T
    grid_tables, grid_masks = [], []
    for c in range(2):
        corner = [((GRID - 1) / 2.0 - BASE) - attr_rows[1 + k : 2 + k, 128 * c : 128 * c + 128] for k in range(3)]
        push = [back_t[8 * c + n : 8 * c + n + 1, :] for n in range(3)]
        lever = cross(corner, push)
        twist = [back_t[8 * c + 3 + n : 8 * c + 4 + n, :] - lever[n] for n in range(3)]
        grid_tables.append(stack(push + twist))
        grid_masks.append(attr_rows[0:1, 128 * c : 128 * c + 128])
    grid_load = per_grain(grid_tables, grid_masks)

    def turn(first):
        v = [grid_load[first + k : first + k + 1, 0:GRAINS] for k in range(3)]
        return [rot[3 * m] * v[0] + rot[3 * m + 1] * v[1] + rot[3 * m + 2] * v[2] for m in range(3)]

    force, torque = turn(0), turn(3)
    force = [node_load[m : m + 1, 0:GRAINS] - force[m] for m in range(3)]
    torque = [node_load[3 + m : 4 + m, 0:GRAINS] - torque[m] for m in range(3)]
    mass = mass_ref[...]
    gain = time_step / mass
    spin_gain = time_step / (0.4 * mass * (3.0 * GRID / 16.0) ** 2)
    vel = [velocity_ref[m : m + 1, :] + force[m] * gain for m in range(3)]
    spin = [spin_ref[m : m + 1, :] + torque[m] * spin_gain for m in range(3)]
    for m in range(3):
        new_velocity_ref[m : m + 1, :] = vel[m]
        new_spin_ref[m : m + 1, :] = spin[m]
        new_position_ref[m : m + 1, :] = pos[m] + time_step * vel[m]
    vec = (x, y, z)
    turned = cross(spin, vec)
    quarter = 0.5 * time_step
    q = [w - quarter * (spin[0] * x + spin[1] * y + spin[2] * z)]
    q += [vec[m] + quarter * (w * spin[m] + turned[m]) for m in range(3)]
    norm = jnp.sqrt(q[0] * q[0] + q[1] * q[1] + q[2] * q[2] + q[3] * q[3])
    for k in range(4):
        new_quaternion_ref[k : k + 1, :] = q[k] / norm

    def finish(e, _):
        @pl.when(e != d)
        def _():
            message(e, d).wait_send()
            reply(e, d).wait_send()

        return 0

    lax.fori_loop(0, DEVS, finish, 0)
    cross_message.wait_send()
    cross_reply.wait_send()


ROWS = 6
SMALL = 13
SCRATCH = 24


def body(
    level_set, node_coords, position, quaternion, velocity, spin, mass, grid_slot, brick_anchor, node_slot, grid_cross,
    anchor_cross, node_cross,
):
    vmem = pl.BlockSpec(memory_space=pltpu.VMEM)
    dma = pltpu.SemaphoreType.DMA
    row = lambda a: a.reshape(1, -1)
    small = (
        node_coords, position, quaternion, velocity, spin, row(mass), row(grid_slot), brick_anchor, row(node_slot),
        row(grid_cross), anchor_cross, row(node_cross), jnp.asarray(spread_matrix(), bf16),
    )
    outs = pl.pallas_call(
        kernel,
        out_shape=[jax.ShapeDtypeStruct((n, GRAINS), f32) for n in (3, 4, 3, 3)],
        in_specs=[pl.BlockSpec(memory_space=pl.ANY)] * (1 + SMALL),
        out_specs=[vmem] * 4,
        scratch_shapes=[
            pltpu.VMEM((GRAINS, SPAN, 32, GRID), bf16),
            pltpu.VMEM((128, 256), f32),
            pltpu.VMEM((256, 128), f32),
            pltpu.VMEM((384, 128), f32),
            pltpu.VMEM((128, 128), f32),
            pltpu.VMEM((128, NODES), bf16),
            pltpu.VMEM((8 * TILES, 128), i32),
            pltpu.VMEM((8 * TILES, 128), i32),
            pltpu.VMEM((256, 128), f32),
            pltpu.VMEM((128, 128), f32),
            pltpu.VMEM((TILES, 1, 128), f32),
            pltpu.VMEM((TILES, 1, 128), f32),
            pltpu.VMEM((128, 128), f32),
            dma,
            dma((DEVS,)),
            dma((DEVS,)),
            dma((DEVS,)),
            dma((DEVS,)),
            dma((4,)),
            dma((SMALL,)),
        ]
        + [pltpu.VMEM(a.shape, a.dtype) for a in small],
        compiler_params=pltpu.CompilerParams(
            collective_id=0, has_side_effects=True, vmem_limit_bytes=60 * 1024 * 1024
        ),
    )(level_set, *small)
    return tuple(outs)


def solution(mesh):
    both = ("group", "dev")
    wide, flat = P(None, both), P(both)
    in_specs = (
        P(both, None, None, None), P(None, both, None), wide, wide, wide, wide, flat, flat, wide, flat, flat, wide, flat,
    )
    return jax.shard_map(body, mesh=mesh, in_specs=in_specs, out_specs=(wide,) * 4, check_vma=False)
```

```python
import jax
import jax.numpy as jnp
from jax import lax
from jax.experimental import pallas as pl
from jax.experimental.pallas import tpu as pltpu
from jax.sharding import PartitionSpec as P

MESH = pl.DeviceIdType.MESH
f32, bf16, i32 = jnp.float32, jnp.bfloat16, jnp.int32

GRID = 64
GROUPS = 8
DEVS = 64
GRAINS = 4
NODES = 512
BASE = GRID // 2 - 5
SPAN = 10
TILES = DEVS + 8
PAIRS = 2 * TILES
LEVELS = 32766.0
stiffness = 0.1
time_step = 0.5
R_PART = (0, 0, 1, 1)
P_PART = (0, 1, 0, 1)


def iota(shape, dim):
    return lax.broadcasted_iota(i32, shape, dim)


def parts(x):
    first = x.astype(bf16)
    rest = x - first.astype(f32)
    second = rest.astype(bf16)
    third = (rest - second.astype(f32)).astype(bf16)
    return first, second, third


def matmul(a, b):
    return jnp.dot(a, b, preferred_element_type=f32)


def matmul_nt(a, b):
    return lax.dot_general(a, b, (((1,), (1,)), ((), ())), preferred_element_type=f32)


def hat(t):
    return jnp.maximum(1.0 - jnp.abs(t), 0.0)


def slope(t):
    return jnp.maximum(jnp.minimum(-2.0 * t, jnp.maximum(t + 1.5, 0.0)), jnp.minimum(t - 1.5, 0.0))


def take(table, index):
    return jnp.take_along_axis(table, index, axis=1, mode="promise_in_bounds")


def near(u):
    r = jnp.floor(u + 0.5)
    f = u - r
    e = jnp.abs(f)
    up = f >= 0.0
    half = jnp.where(up, 0.5, -0.5)
    step = jnp.where(up, 1, -1)
    a = r.astype(i32)
    b = a + step
    c = a - step
    in_a, in_b, in_c = ((i & -8) == 0 for i in (a, b, c))
    hats = (jnp.where(in_a, 1.0 - e, 0.0), jnp.where(in_b, e, 0.0))
    slopes = (
        jnp.where(in_a, -2.0 * f, 0.0),
        jnp.where(in_b, f + half, 0.0),
        jnp.where(in_c, f - half, 0.0),
    )
    return (a & 7, b & 7, c & 7), hats, slopes


def contact(even, odd, scale, u):
    rx = jnp.floor(u[0] + 0.5).astype(i32)
    bit_e = ((rx + 1) << 4) & 64
    bit_o = ((rx - 1) << 4) & 64
    de = u[0] - (bit_e >> 4).astype(f32)
    do = u[0] - (bit_o >> 4).astype(f32) - 2.0
    tiny = 1.0 / 65536.0

    def lanes(weight):
        hi_e, hi_o = weight(de - 1.0) * tiny, weight(do - 1.0) * tiny
        return weight(de) - hi_e, hi_e, weight(do) - hi_o, hi_o

    hx, sx = lanes(hat), lanes(slope)
    yi, hy, sy = near(u[1])
    zi, hz, sz = near(u[2])
    yi = [i << 3 for i in yi]

    def column(j, k, with_slope):
        place = yi[j] | zi[k]
        we, wo = take(even, bit_e | place), take(odd, bit_o | place)
        values = (((we << 16) >> 16).astype(f32), we.astype(f32), ((wo << 16) >> 16).astype(f32), wo.astype(f32))

        def meet(w):
            return (values[0] * w[0] + values[1] * w[1]) + (values[2] * w[2] + values[3] * w[3])

        return meet(hx), (meet(sx) if with_slope else None)

    rows, rows_x, rows_z = [], [], []
    for j in range(2):
        v0, s0 = column(j, 0, True)
        v1, s1 = column(j, 1, True)
        v2, _ = column(j, 2, False)
        rows.append(v0 * hz[0] + v1 * hz[1])
        rows_x.append(s0 * hz[0] + s1 * hz[1])
        rows_z.append(v0 * sz[0] + v1 * sz[1] + v2 * sz[2])
    v0, _ = column(2, 0, False)
    v1, _ = column(2, 1, False)
    rows.append(v0 * hz[0] + v1 * hz[1])
    phi = (rows[0] * hy[0] + rows[1] * hy[1]) * scale
    gx = (rows_x[0] * hy[0] + rows_x[1] * hy[1]) * scale
    gy = (rows[0] * sy[0] + rows[1] * sy[1] + rows[2] * sy[2]) * scale
    gz = (rows_z[0] * hy[0] + rows_z[1] * hy[1]) * scale
    push = stiffness * jnp.maximum(-phi, 0.0) * lax.rsqrt(jnp.maximum(gx * gx + gy * gy + gz * gz, 1.0))
    g = (gx * push, gy * push, gz * push)
    return g + cross(u, g)


def cross(a, b):
    return (a[1] * b[2] - a[2] * b[1], a[2] * b[0] - a[0] * b[2], a[0] * b[1] - a[1] * b[0])


def kernel(
    level_ref, *refs
):
    sources, refs = refs[:SMALL], refs[SMALL:]
    (
        new_position_ref, new_quaternion_ref, new_velocity_ref, new_spin_ref,
        window, attr, cols, slab, pose, points, out_msg, in_msg, metas, sums, back,
        window_sem, send_sem, recv_sem, ret_send_sem, ret_recv_sem, cross_sem, input_sem,
    ) = refs[:SCRATCH]
    inputs = refs[SCRATCH:]
    (
        coords_ref, position_ref, quaternion_ref, velocity_ref, spin_ref, mass_ref, grid_ref, anchor_ref, node_ref,
        grid_cross_ref, anchor_cross_ref, node_cross_ref,
    ) = inputs
    g = lax.axis_index("group")
    d = lax.axis_index("dev")
    up, down = lax.rem(g + 1, GROUPS), lax.rem(g + GROUPS - 1, GROUPS)
    barrier = pltpu.get_barrier_semaphore()

    def greet(k, _):
        e = lax.rem(d + k, DEVS)
        pl.semaphore_signal(barrier, inc=1, device_id=(g, e), device_id_type=MESH)
        return 0

    load = pltpu.make_async_copy(
        level_ref.at[:, BASE : BASE + SPAN, 16:48, :], window, window_sem
    )
    load.start()
    fetches = [
        pltpu.make_async_copy(source, target, input_sem.at[n])
        for n, (source, target) in enumerate(zip(sources, inputs))
    ]
    for fetch in fetches:
        fetch.start()
    lax.fori_loop(1, DEVS, greet, 0, unroll=7)
    for other in (up, down):
        pl.semaphore_signal(barrier, inc=1, device_id=(other, d), device_id_type=MESH)

    for fetch in fetches:
        fetch.wait()

    attr[...] = jnp.zeros_like(attr)
    attr[0:1, 0:128] = (grid_ref[...] + 1).astype(f32)
    attr[0:1, 128:144] = (grid_cross_ref[...] + 1).astype(f32)
    attr[1:4, 0:128] = (anchor_ref[...] - BASE).astype(f32)
    attr[1:4, 128:144] = (anchor_cross_ref[...] - BASE).astype(f32)
    attr[4:5, 0:128] = (node_ref[...] + 1).astype(f32)
    attr[4:5, 128:144] = (node_cross_ref[...] + 1).astype(f32)
    slot_to = iota((256, 256), 0)
    order = (iota((256, 256), 1) == ((slot_to & 127) << 1) + (slot_to >> 7)).astype(f32).astype(bf16)
    attr_b = attr[...].astype(bf16)
    cols[...] = matmul_nt(order, attr_b)

    w, x, y, z = (quaternion_ref[k : k + 1, :] for k in range(4))
    rot = (
        1.0 - 2.0 * (y * y + z * z), 2.0 * (x * y - w * z), 2.0 * (x * z + w * y),
        2.0 * (x * y + w * z), 1.0 - 2.0 * (x * x + z * z), 2.0 * (y * z - w * x),
        2.0 * (x * z - w * y), 2.0 * (y * z + w * x), 1.0 - 2.0 * (x * x + y * y),
    )
    pos = [position_ref[m : m + 1, :] for m in range(3)]
    pose[...] = jnp.zeros_like(pose)
    for k in range(3):
        turned = rot[k] * pos[0] + rot[3 + k] * pos[1] + rot[6 + k] * pos[2]
        for half in (0, 64):
            at = half + 16 * k
            for m in range(3):
                pose[at + 4 * m : at + 4 * m + 4, 0:GRAINS] = jnp.broadcast_to(rot[3 * m + k], (4, GRAINS))
            pose[at + 12 : at + 13, 0:GRAINS] = ((GRID - 1) / 2.0 - BASE) - turned
            pose[at + 14 : at + 15, 0:GRAINS] = pos[k]
    pose_cols = pose[...].T

    lane64 = iota((64, 384), 1)
    select_z = (iota((64, 384), 0) == BASE + (lane64 >> 7) + (lane64 & 7)).astype(f32).astype(bf16)
    place_y = iota((16, 128), 0)
    lane_y = (iota((16, 128), 1) >> 3) & 7
    load.wait()
    planes = matmul(window[...].reshape(GRAINS * SPAN * 32, GRID), select_z)
    planes = planes.reshape(GRAINS * SPAN, 32, 384)[:, 8:24, :]
    low_half = iota((40, 128), 1) < 64
    for ay in range(3):
        keep = (place_y == BASE - 24 + ay + lane_y).astype(f32)
        for az in range(3):
            picked = jnp.sum(planes[:, :, 128 * az : 128 * az + 128] * keep[None], axis=1)
            q = 3 * ay + az
            slab[40 * q : 40 * q + 40, :] = jnp.where(low_half, picked, pltpu.roll(picked, 36, 0))
    slab[360:384, :] = jnp.zeros((24, 128), f32)
    code = [
        (cols[128 * c : 128 * c + TILES, 2:3] * 3.0 + cols[128 * c : 128 * c + TILES, 3:4]) * 40.0
        + (cols[128 * c : 128 * c + TILES, 0:1] - 1.0) * 10.0
        + cols[128 * c : 128 * c + TILES, 1:2]
        for c in range(2)
    ]
    code = jnp.concatenate([code[c] + float(j) for c in range(2) for j in range(4)], axis=0).astype(i32)
    pick = (iota((8 * TILES, 384), 1) == code).astype(f32).astype(bf16)
    bricks = matmul(pick, slab[...].astype(bf16))
    lane = iota((TILES, 128), 1)
    pose_parts = parts(pose_cols)
    lane_f = lane & 15
    unit = jnp.where(
        lane_f < 12, 2.0**30, jnp.where(lane_f == 12, 2.0**27, jnp.where(lane_f == 13, 2.0**28, 0.0))
    )
    halves = []
    for c in range(2):
        rows = [bricks[TILES * (4 * c + j) : TILES * (4 * c + j + 1), :] for j in range(4)]
        most = jnp.maximum(
            jnp.maximum(jnp.abs(rows[0]), jnp.abs(rows[1])), jnp.maximum(jnp.abs(rows[2]), jnp.abs(rows[3]))
        )
        most = jnp.maximum(jnp.max(most, axis=1, keepdims=True), 1e-6)
        inverse = LEVELS / most
        level = [jnp.floor(row * inverse + 0.5).astype(i32) for row in rows]
        out_msg[pl.ds(2 * c, TILES, stride=8), :] = (level[1] << 16) + level[0]
        out_msg[pl.ds(2 * c + 1, TILES, stride=8), :] = (level[3] << 16) + level[2]
        own = cols[128 * c : 128 * c + TILES, :]
        grain = (own[:, 0:1].astype(i32) - 1 == lane).astype(f32).astype(bf16)
        meta = matmul(grain, pose_parts[0]) + matmul(grain, pose_parts[1]) + matmul(grain, pose_parts[2])
        for k in range(3):
            meta = meta - jnp.where(lane == 64 * c + 16 * k + 12, own[:, 1 + k : 2 + k], 0.0)
        halves.append(jnp.where(lane_f == 13, most, meta))
    out_msg[pl.ds(4, TILES, stride=8), :] = (jnp.where(lane < 64, halves[0], halves[1]) * unit).astype(i32)

    def message(e, other):
        return pltpu.make_async_remote_copy(
            src_ref=out_msg.at[pl.ds(pl.multiple_of(8 * e, 8), ROWS)],
            dst_ref=in_msg.at[pl.ds(pl.multiple_of(8 * other, 8), ROWS)],
            send_sem=send_sem,
            recv_sem=recv_sem.at[other // 8],
            device_id=(g, e),
            device_id_type=MESH,
        )

    def messages(count, octet):
        return pltpu.make_async_remote_copy(
            src_ref=out_msg.at[pl.ds(0, ROWS * count)],
            dst_ref=in_msg.at[pl.ds(0, ROWS * count)],
            send_sem=send_sem,
            recv_sem=recv_sem.at[octet],
            device_id=(up, d),
            device_id_type=MESH,
        )

    def reply(e, other):
        return pltpu.make_async_remote_copy(
            src_ref=sums.at[pl.ds(e, 1)],
            dst_ref=back.at[pl.ds(other, 1)],
            send_sem=ret_send_sem,
            recv_sem=ret_recv_sem,
            device_id=(g, e),
            device_id_type=MESH,
        )

    def replies(count):
        return pltpu.make_async_remote_copy(
            src_ref=sums.at[pl.ds(0, count)],
            dst_ref=back.at[pl.ds(0, count)],
            send_sem=ret_send_sem,
            recv_sem=ret_recv_sem,
            device_id=(up, d),
            device_id_type=MESH,
        )

    cross_message = pltpu.make_async_remote_copy(
        src_ref=out_msg.at[pl.ds(8 * DEVS, 64)],
        dst_ref=in_msg.at[pl.ds(8 * DEVS, 64)],
        send_sem=cross_sem.at[0],
        recv_sem=cross_sem.at[1],
        device_id=(up, d),
        device_id_type=MESH,
    )
    cross_reply = pltpu.make_async_remote_copy(
        src_ref=sums.at[pl.ds(DEVS, 8)],
        dst_ref=back.at[pl.ds(DEVS, 8)],
        send_sem=cross_sem.at[2],
        recv_sem=cross_sem.at[3],
        device_id=(down, d),
        device_id_type=MESH,
    )
    own = d // 8
    own_rows = pl.ds(pl.multiple_of(8 * d, 8), ROWS)
    own_message = pltpu.make_async_copy(out_msg.at[own_rows], in_msg.at[own_rows], recv_sem.at[own])
    own_reply = pltpu.make_async_copy(sums.at[pl.ds(d, 1)], back.at[pl.ds(d, 1)], ret_recv_sem)

    def octet(t):
        far = (t + 1) // 2
        shift = jnp.where(t % 2 == 1, far, 8 - far)
        return (own + shift) % 8

    metas[...] = jnp.zeros_like(metas)
    sums[...] = jnp.zeros_like(sums)
    back[TILES:128, :] = jnp.zeros((128 - TILES, 128), f32)
    pl.semaphore_wait(barrier, DEVS + 1)
    own_message.start()
    for i in range(1, 8):
        message(8 * own + (d + i) % 8, d).start()
    cross_message.start()

    def send_octet(t, _):
        base = 8 * octet(t)
        for i in range(8):
            message(base + (d + i) % 8, d).start()
        return 0

    lax.fori_loop(1, 8, send_octet, 0)

    world = []
    for m in range(3):
        p = pose_cols[0:GRAINS, 16 * m + 14 : 16 * m + 15]
        for n in range(3):
            lane_r = 16 * n + 4 * m
            p = p + pose_cols[0:GRAINS, lane_r : lane_r + 1] * coords_ref[n]
        world.append(p)
    ones = jnp.where(iota((GRAINS, NODES), 0) == 0, 1.0, 0.0)
    world = parts(jnp.concatenate(world + [ones], axis=0))
    for combo, part in enumerate(P_PART):
        for block in range(8):
            points[128 * combo + 16 * block : 128 * combo + 16 * block + 16, :] = world[part]
    attr_rows = matmul_nt(attr_b, order)
    lane8 = iota((8, 128), 1)
    lane8_f = lane8 & 15
    per_lane = jnp.where(
        lane8_f < 12, 2.0**-30, jnp.where(lane8_f == 12, 2.0**-27, jnp.where(lane8_f == 13, 2.0**-28 / LEVELS, 0.0))
    )

    def work(t, _):
        is_cross = t == 1
        vg = jnp.where(is_cross, 8, octet(jnp.where(t > 1, t - 1, 0)))

        @pl.when(is_cross)
        def _():
            cross_message.wait_recv()

        @pl.when(t != 1)
        def _():
            messages(8, vg).wait_recv()

        at = pl.multiple_of(64 * vg, 64)
        meta = in_msg[pl.ds(at + 4, 8, stride=8), :].astype(f32) * per_lane
        metas[pl.ds(pl.multiple_of(8 * vg, 8), 8), :] = meta
        node = [cols[pl.ds(pl.multiple_of(128 * c + 8 * vg, 8), 8), :][:, 4:5] for c in range(2)]
        mine = [jnp.logical_or((lane8 & 3) == node[c].astype(i32) - 1, lane8_f == 12) for c in range(2)]
        left = [
            jnp.where(jnp.logical_and(mine[c], (lane8 >> 4) == 4 * c + k), meta, 0.0) for k in range(3) for c in range(2)
        ]
        left = parts(jnp.concatenate(left, axis=0))
        place = matmul(jnp.concatenate([left[part] for part in R_PART], axis=1), points[...])
        result = jnp.zeros((8, 128), f32)
        for c in range(2):
            even = in_msg[pl.ds(at + 2 * c, 8, stride=8), :]
            odd = in_msg[pl.ds(at + 2 * c + 1, 8, stride=8), :]
            scale = jnp.broadcast_to(jnp.where(node[c] > 0.5, meta[:, 64 * c + 13 : 64 * c + 14], 0.0), (8, 128))
            total = None
            for chunk in range(NODES // 128):
                u = tuple(place[16 * k + 8 * c : 16 * k + 8 * c + 8, 128 * chunk : 128 * chunk + 128] for k in range(3))
                term = contact(even, odd, scale, u)
                total = term if total is None else tuple(a + b for a, b in zip(total, term))
            for n in range(6):
                result = jnp.where(lane8 == 8 * c + n, jnp.sum(total[n], axis=1, keepdims=True), result)
        sums[pl.ds(pl.multiple_of(8 * vg, 8), 8), :] = result

        @pl.when(is_cross)
        def _():
            cross_reply.start()

        @pl.when(t == 0)
        def _():
            own_reply.start()
            for i in range(1, 8):
                reply(8 * vg + (d + i) % 8, d).start()

        @pl.when(t > 1)
        def _():
            for i in range(8):
                reply(8 * vg + (d + i) % 8, d).start()

        return 0

    lax.fori_loop(0, 9, work, 0)

    sums_t = sums[...].T
    lane_p = iota((8, 128), 1)
    row_p = iota((8, 128), 0)

    def per_grain(tables, masks):
        out = jnp.zeros((8, 128), f32)
        for grain in range(GRAINS):
            kept = sum(jnp.where(masks[c] == grain + 1.0, tables[c], 0.0) for c in range(2))
            out = jnp.where(lane_p == grain, jnp.sum(kept, axis=1, keepdims=True), out)
        return out

    def stack(rows):
        out = jnp.zeros((8, 128), f32)
        for n, row in enumerate(rows):
            out = jnp.where(row_p == n, row, out)
        return out

    meta_t = metas[...].T
    node_tables, node_masks = [], []
    for c in range(2):
        at = 64 * c
        r = [[meta_t[at + 16 * k + 4 * m : at + 16 * k + 4 * m + 1, :] for k in range(3)] for m in range(3)]
        mask = attr_rows[4:5, 128 * c : 128 * c + 128]
        centre = []
        for m in range(3):
            value = jnp.zeros((1, 128), f32)
            for grain in range(GRAINS):
                value = jnp.where(mask == grain + 1.0, pose[16 * m + 14 : 16 * m + 15, grain : grain + 1], value)
            centre.append(value)
        shift = [
            r[0][k] * centre[0] + r[1][k] * centre[1] + r[2][k] * centre[2] + meta_t[at + 16 * k + 12 : at + 16 * k + 13, :]
            for k in range(3)
        ]
        push = [sums_t[8 * c + n : 8 * c + n + 1, :] for n in range(3)]
        twist = [sums_t[8 * c + 3 + n : 8 * c + 4 + n, :] for n in range(3)]
        lever = cross(shift, push)
        twist = [twist[n] - lever[n] for n in range(3)]
        rows = [r[m][0] * v[0] + r[m][1] * v[1] + r[m][2] * v[2] for v in (push, twist) for m in range(3)]
        node_tables.append(stack(rows))
        node_masks.append(mask)
    node_load = per_grain(node_tables, node_masks)

    replies(DEVS).wait_recv()
    cross_reply.wait_recv()
    back_t = back[...].T
    grid_tables, grid_masks = [], []
    for c in range(2):
        corner = [((GRID - 1) / 2.0 - BASE) - attr_rows[1 + k : 2 + k, 128 * c : 128 * c + 128] for k in range(3)]
        push = [back_t[8 * c + n : 8 * c + n + 1, :] for n in range(3)]
        lever = cross(corner, push)
        twist = [back_t[8 * c + 3 + n : 8 * c + 4 + n, :] - lever[n] for n in range(3)]
        grid_tables.append(stack(push + twist))
        grid_masks.append(attr_rows[0:1, 128 * c : 128 * c + 128])
    grid_load = per_grain(grid_tables, grid_masks)

    def turn(first):
        v = [grid_load[first + k : first + k + 1, 0:GRAINS] for k in range(3)]
        return [rot[3 * m] * v[0] + rot[3 * m + 1] * v[1] + rot[3 * m + 2] * v[2] for m in range(3)]

    force, torque = turn(0), turn(3)
    force = [node_load[m : m + 1, 0:GRAINS] - force[m] for m in range(3)]
    torque = [node_load[3 + m : 4 + m, 0:GRAINS] - torque[m] for m in range(3)]
    mass = mass_ref[...]
    gain = time_step / mass
    spin_gain = time_step / (0.4 * mass * (3.0 * GRID / 16.0) ** 2)
    vel = [velocity_ref[m : m + 1, :] + force[m] * gain for m in range(3)]
    spin = [spin_ref[m : m + 1, :] + torque[m] * spin_gain for m in range(3)]
    for m in range(3):
        new_velocity_ref[m : m + 1, :] = vel[m]
        new_spin_ref[m : m + 1, :] = spin[m]
        new_position_ref[m : m + 1, :] = pos[m] + time_step * vel[m]
    vec = (x, y, z)
    turned = cross(spin, vec)
    quarter = 0.5 * time_step
    q = [w - quarter * (spin[0] * x + spin[1] * y + spin[2] * z)]
    q += [vec[m] + quarter * (w * spin[m] + turned[m]) for m in range(3)]
    norm = jnp.sqrt(q[0] * q[0] + q[1] * q[1] + q[2] * q[2] + q[3] * q[3])
    for k in range(4):
        new_quaternion_ref[k : k + 1, :] = q[k] / norm

    messages(DEVS - 1, 0).wait_send()
    replies(DEVS - 1).wait_send()
    cross_message.wait_send()
    cross_reply.wait_send()


ROWS = 5
SMALL = 12
SCRATCH = 22


def settle_kernel(*refs):
    sem = refs[8]
    copies = [pltpu.make_async_copy(refs[n], refs[4 + n], sem.at[n]) for n in range(4)]
    for copy in copies:
        copy.start()
    for copy in copies:
        copy.wait()


def settle(outs):
    anywhere = pl.BlockSpec(memory_space=pl.ANY)
    return pl.pallas_call(
        settle_kernel,
        out_shape=[jax.ShapeDtypeStruct(a.shape, a.dtype) for a in outs],
        in_specs=[anywhere] * 4,
        out_specs=[anywhere] * 4,
        scratch_shapes=[pltpu.SemaphoreType.DMA((4,))],
    )(*outs)


def body(
    level_set, node_coords, position, quaternion, velocity, spin, mass, grid_slot, brick_anchor, node_slot, grid_cross,
    anchor_cross, node_cross,
):
    vmem = pl.BlockSpec(memory_space=pltpu.VMEM)
    dma = pltpu.SemaphoreType.DMA
    row = lambda a: a.reshape(1, -1)
    small = (
        node_coords, position, quaternion, velocity, spin, row(mass), row(grid_slot), brick_anchor, row(node_slot),
        row(grid_cross), anchor_cross, row(node_cross),
    )
    outs = pl.pallas_call(
        kernel,
        out_shape=[jax.ShapeDtypeStruct((n, GRAINS), f32) for n in (3, 4, 3, 3)],
        in_specs=[pl.BlockSpec(memory_space=pl.ANY)] * (1 + SMALL),
        out_specs=[vmem] * 4,
        scratch_shapes=[
            pltpu.VMEM((GRAINS, SPAN, 32, GRID), bf16),
            pltpu.VMEM((128, 256), f32),
            pltpu.VMEM((256, 128), f32),
            pltpu.VMEM((384, 128), f32),
            pltpu.VMEM((128, 128), f32),
            pltpu.VMEM((128 * len(P_PART), NODES), bf16),
            pltpu.VMEM((8 * TILES, 128), i32),
            pltpu.VMEM((8 * TILES, 128), i32),
            pltpu.VMEM((128, 128), f32),
            pltpu.VMEM((128, 128), f32),
            pltpu.VMEM((128, 128), f32),
            dma,
            dma,
            dma((8,)),
            dma,
            dma,
            dma((4,)),
            dma((SMALL,)),
        ]
        + [pltpu.VMEM(a.shape, a.dtype) for a in small],
        compiler_params=pltpu.CompilerParams(
            collective_id=0, has_side_effects=True, vmem_limit_bytes=60 * 1024 * 1024
        ),
    )(level_set, *small)
    return tuple(settle(outs))


def solution(mesh):
    both = ("group", "dev")
    wide, flat = P(None, both), P(both)
    in_specs = (
        P(both, None, None, None), P(None, both, None), wide, wide, wide, wide, flat, flat, wide, flat, flat, wide, flat,
    )
    return jax.shard_map(body, mesh=mesh, in_specs=in_specs, out_specs=(wide,) * 4, check_vma=False)
```

```python
import jax
import jax.numpy as jnp
from jax import lax
from jax.experimental import pallas as pl
from jax.experimental.pallas import tpu as pltpu
from jax.sharding import PartitionSpec as P

MESH = pl.DeviceIdType.MESH
f32, bf16, i32 = jnp.float32, jnp.bfloat16, jnp.int32

GRID = 64
GROUPS = 8
DEVS = 64
GRAINS = 4
NODES = 512
BASE = GRID // 2 - 5
SPAN = 10
TILES = DEVS + 8
PAIRS = 2 * TILES
LEVELS = 32766.0
stiffness = 0.1
time_step = 0.5
R_PART = (0, 0, 1, 1)
P_PART = (0, 1, 0, 1)


def iota(shape, dim):
    return lax.broadcasted_iota(i32, shape, dim)


def parts(x):
    first = x.astype(bf16)
    rest = x - first.astype(f32)
    second = rest.astype(bf16)
    third = (rest - second.astype(f32)).astype(bf16)
    return first, second, third


def matmul(a, b):
    return jnp.dot(a, b, preferred_element_type=f32)


def matmul_nt(a, b):
    return lax.dot_general(a, b, (((1,), (1,)), ((), ())), preferred_element_type=f32)


def hat(t):
    return jnp.maximum(1.0 - jnp.abs(t), 0.0)


def slope(t):
    return jnp.maximum(jnp.minimum(-2.0 * t, jnp.maximum(t + 1.5, 0.0)), jnp.minimum(t - 1.5, 0.0))


def take(table, index):
    return jnp.take_along_axis(table, index, axis=1, mode="promise_in_bounds")


def near(u):
    r = jnp.floor(u + 0.5)
    f = u - r
    e = jnp.abs(f)
    up = f >= 0.0
    half = jnp.where(up, 0.5, -0.5)
    step = jnp.where(up, 1, -1)
    a = r.astype(i32)
    b = a + step
    c = a - step
    in_a, in_b, in_c = ((i & -8) == 0 for i in (a, b, c))
    hats = (jnp.where(in_a, 1.0 - e, 0.0), jnp.where(in_b, e, 0.0))
    slopes = (
        jnp.where(in_a, -2.0 * f, 0.0),
        jnp.where(in_b, f + half, 0.0),
        jnp.where(in_c, f - half, 0.0),
    )
    return (a & 7, b & 7, c & 7), hats, slopes


def contact(even, odd, scale, u):
    rx = jnp.floor(u[0] + 0.5).astype(i32)
    bit_e = ((rx + 1) << 4) & 64
    bit_o = ((rx - 1) << 4) & 64
    de = u[0] - (bit_e >> 4).astype(f32)
    do = u[0] - (bit_o >> 4).astype(f32) - 2.0
    tiny = 1.0 / 65536.0

    def lanes(weight):
        hi_e, hi_o = weight(de - 1.0) * tiny, weight(do - 1.0) * tiny
        return weight(de) - hi_e, hi_e, weight(do) - hi_o, hi_o

    hx, sx = lanes(hat), lanes(slope)
    yi, hy, sy = near(u[1])
    zi, hz, sz = near(u[2])
    yi = [i << 3 for i in yi]

    def column(j, k, with_slope):
        place = yi[j] | zi[k]
        we, wo = take(even, bit_e | place), take(odd, bit_o | place)
        values = (((we << 16) >> 16).astype(f32), we.astype(f32), ((wo << 16) >> 16).astype(f32), wo.astype(f32))

        def meet(w):
            return (values[0] * w[0] + values[1] * w[1]) + (values[2] * w[2] + values[3] * w[3])

        return meet(hx), (meet(sx) if with_slope else None)

    rows, rows_x, rows_z = [], [], []
    for j in range(2):
        v0, s0 = column(j, 0, True)
        v1, s1 = column(j, 1, True)
        v2, _ = column(j, 2, False)
        rows.append(v0 * hz[0] + v1 * hz[1])
        rows_x.append(s0 * hz[0] + s1 * hz[1])
        rows_z.append(v0 * sz[0] + v1 * sz[1] + v2 * sz[2])
    v0, _ = column(2, 0, False)
    v1, _ = column(2, 1, False)
    rows.append(v0 * hz[0] + v1 * hz[1])
    phi = (rows[0] * hy[0] + rows[1] * hy[1]) * scale
    gx = (rows_x[0] * hy[0] + rows_x[1] * hy[1]) * scale
    gy = (rows[0] * sy[0] + rows[1] * sy[1] + rows[2] * sy[2]) * scale
    gz = (rows_z[0] * hy[0] + rows_z[1] * hy[1]) * scale
    push = stiffness * jnp.maximum(-phi, 0.0) * lax.rsqrt(jnp.maximum(gx * gx + gy * gy + gz * gz, 1.0))
    g = (gx * push, gy * push, gz * push)
    return g + cross(u, g)


def cross(a, b):
    return (a[1] * b[2] - a[2] * b[1], a[2] * b[0] - a[0] * b[2], a[0] * b[1] - a[1] * b[0])


def kernel(
    level_ref, *refs
):
    sources, refs = refs[:SMALL], refs[SMALL:]
    (
        new_position_ref, new_quaternion_ref, new_velocity_ref, new_spin_ref,
        window, attr, cols, slab, pose, points, out_msg, in_msg, metas, sums, back,
        window_sem, send_sem, recv_sem, ret_send_sem, ret_recv_sem, cross_sem, input_sem,
    ) = refs[:SCRATCH]
    inputs = refs[SCRATCH:]
    (
        coords_ref, position_ref, quaternion_ref, velocity_ref, spin_ref, mass_ref, grid_ref, anchor_ref, node_ref,
        grid_cross_ref, anchor_cross_ref, node_cross_ref,
    ) = inputs
    g = lax.axis_index("group")
    d = lax.axis_index("dev")
    up, down = lax.rem(g + 1, GROUPS), lax.rem(g + GROUPS - 1, GROUPS)
    barrier = pltpu.get_barrier_semaphore()

    def greet(k, _):
        e = lax.rem(d + k, DEVS)
        pl.semaphore_signal(barrier, inc=1, device_id=(g, e), device_id_type=MESH)
        return 0

    load = pltpu.make_async_copy(
        level_ref.at[:, BASE : BASE + SPAN, 16:48, :], window, window_sem
    )
    load.start()
    fetches = [
        pltpu.make_async_copy(source, target, input_sem.at[n])
        for n, (source, target) in enumerate(zip(sources, inputs))
    ]
    for fetch in fetches:
        fetch.start()
    greet(DEVS // 2, 0)

    def greet_two(j, _):
        greet(DEVS // 2 - j, 0)
        return greet(DEVS // 2 + j, 0)

    lax.fori_loop(1, DEVS // 2, greet_two, 0, unroll=4)
    for other in (up, down):
        pl.semaphore_signal(barrier, inc=1, device_id=(other, d), device_id_type=MESH)

    for fetch in fetches:
        fetch.wait()

    attr[...] = jnp.zeros_like(attr)
    attr[0:1, 0:128] = (grid_ref[...] + 1).astype(f32)
    attr[0:1, 128:144] = (grid_cross_ref[...] + 1).astype(f32)
    attr[1:4, 0:128] = (anchor_ref[...] - BASE).astype(f32)
    attr[1:4, 128:144] = (anchor_cross_ref[...] - BASE).astype(f32)
    attr[4:5, 0:128] = (node_ref[...] + 1).astype(f32)
    attr[4:5, 128:144] = (node_cross_ref[...] + 1).astype(f32)
    slot_to = iota((256, 256), 0)
    order = (iota((256, 256), 1) == ((slot_to & 127) << 1) + (slot_to >> 7)).astype(f32).astype(bf16)
    attr_b = attr[...].astype(bf16)
    cols[...] = matmul_nt(order, attr_b)

    w, x, y, z = (quaternion_ref[k : k + 1, :] for k in range(4))
    rot = (
        1.0 - 2.0 * (y * y + z * z), 2.0 * (x * y - w * z), 2.0 * (x * z + w * y),
        2.0 * (x * y + w * z), 1.0 - 2.0 * (x * x + z * z), 2.0 * (y * z - w * x),
        2.0 * (x * z - w * y), 2.0 * (y * z + w * x), 1.0 - 2.0 * (x * x + y * y),
    )
    pos = [position_ref[m : m + 1, :] for m in range(3)]
    pose[...] = jnp.zeros_like(pose)
    for k in range(3):
        turned = rot[k] * pos[0] + rot[3 + k] * pos[1] + rot[6 + k] * pos[2]
        for half in (0, 64):
            at = half + 16 * k
            for m in range(3):
                pose[at + 4 * m : at + 4 * m + 4, 0:GRAINS] = jnp.broadcast_to(rot[3 * m + k], (4, GRAINS))
            pose[at + 12 : at + 13, 0:GRAINS] = ((GRID - 1) / 2.0 - BASE) - turned
            pose[at + 14 : at + 15, 0:GRAINS] = pos[k]
    pose_cols = pose[...].T

    lane64 = iota((64, 384), 1)
    select_z = (iota((64, 384), 0) == BASE + (lane64 >> 7) + (lane64 & 7)).astype(f32).astype(bf16)
    place_y = iota((16, 128), 0)
    lane_y = (iota((16, 128), 1) >> 3) & 7
    load.wait()
    planes = matmul(window[...].reshape(GRAINS * SPAN * 32, GRID), select_z)
    planes = planes.reshape(GRAINS * SPAN, 32, 384)[:, 8:24, :]
    low_half = iota((40, 128), 1) < 64
    for ay in range(3):
        keep = (place_y == BASE - 24 + ay + lane_y).astype(f32)
        for az in range(3):
            picked = jnp.sum(planes[:, :, 128 * az : 128 * az + 128] * keep[None], axis=1)
            q = 3 * ay + az
            slab[40 * q : 40 * q + 40, :] = jnp.where(low_half, picked, pltpu.roll(picked, 36, 0))
    slab[360:384, :] = jnp.zeros((24, 128), f32)
    code = [
        (cols[128 * c : 128 * c + TILES, 2:3] * 3.0 + cols[128 * c : 128 * c + TILES, 3:4]) * 40.0
        + (cols[128 * c : 128 * c + TILES, 0:1] - 1.0) * 10.0
        + cols[128 * c : 128 * c + TILES, 1:2]
        for c in range(2)
    ]
    code = jnp.concatenate([code[c] + float(j) for c in range(2) for j in range(4)], axis=0).astype(i32)
    pick = (iota((8 * TILES, 384), 1) == code).astype(f32).astype(bf16)
    bricks = matmul(pick, slab[...].astype(bf16))
    lane = iota((TILES, 128), 1)
    pose_parts = parts(pose_cols)
    lane_f = lane & 15
    unit = jnp.where(
        lane_f < 12, 2.0**30, jnp.where(lane_f == 12, 2.0**27, jnp.where(lane_f == 13, 2.0**28, 0.0))
    )
    halves = []
    for c in range(2):
        rows = [bricks[TILES * (4 * c + j) : TILES * (4 * c + j + 1), :] for j in range(4)]
        most = jnp.maximum(
            jnp.maximum(jnp.abs(rows[0]), jnp.abs(rows[1])), jnp.maximum(jnp.abs(rows[2]), jnp.abs(rows[3]))
        )
        most = jnp.maximum(jnp.max(most, axis=1, keepdims=True), 1e-6)
        inverse = LEVELS / most
        level = [jnp.floor(row * inverse + 0.5).astype(i32) for row in rows]
        out_msg[pl.ds(2 * c, TILES, stride=8), :] = (level[1] << 16) + level[0]
        out_msg[pl.ds(2 * c + 1, TILES, stride=8), :] = (level[3] << 16) + level[2]
        own = cols[128 * c : 128 * c + TILES, :]
        grain = (own[:, 0:1].astype(i32) - 1 == lane).astype(f32).astype(bf16)
        meta = matmul(grain, pose_parts[0]) + matmul(grain, pose_parts[1]) + matmul(grain, pose_parts[2])
        for k in range(3):
            meta = meta - jnp.where(lane == 64 * c + 16 * k + 12, own[:, 1 + k : 2 + k], 0.0)
        halves.append(jnp.where(lane_f == 13, most, meta))
    out_msg[pl.ds(4, TILES, stride=8), :] = (jnp.where(lane < 64, halves[0], halves[1]) * unit).astype(i32)

    def message(e, other):
        return pltpu.make_async_remote_copy(
            src_ref=out_msg.at[pl.ds(pl.multiple_of(8 * e, 8), ROWS)],
            dst_ref=in_msg.at[pl.ds(pl.multiple_of(8 * other, 8), ROWS)],
            send_sem=send_sem,
            recv_sem=recv_sem.at[other // 8],
            device_id=(g, e),
            device_id_type=MESH,
        )

    def messages(count, octet):
        return pltpu.make_async_remote_copy(
            src_ref=out_msg.at[pl.ds(0, ROWS * count)],
            dst_ref=in_msg.at[pl.ds(0, ROWS * count)],
            send_sem=send_sem,
            recv_sem=recv_sem.at[octet],
            device_id=(up, d),
            device_id_type=MESH,
        )

    def reply(e, other):
        return pltpu.make_async_remote_copy(
            src_ref=sums.at[pl.ds(e, 1)],
            dst_ref=back.at[pl.ds(other, 1)],
            send_sem=ret_send_sem,
            recv_sem=ret_recv_sem,
            device_id=(g, e),
            device_id_type=MESH,
        )

    def replies(count):
        return pltpu.make_async_remote_copy(
            src_ref=sums.at[pl.ds(0, count)],
            dst_ref=back.at[pl.ds(0, count)],
            send_sem=ret_send_sem,
            recv_sem=ret_recv_sem,
            device_id=(up, d),
            device_id_type=MESH,
        )

    cross_message = pltpu.make_async_remote_copy(
        src_ref=out_msg.at[pl.ds(8 * DEVS, 64)],
        dst_ref=in_msg.at[pl.ds(8 * DEVS, 64)],
        send_sem=cross_sem.at[0],
        recv_sem=cross_sem.at[1],
        device_id=(up, d),
        device_id_type=MESH,
    )
    cross_reply = pltpu.make_async_remote_copy(
        src_ref=sums.at[pl.ds(DEVS, 8)],
        dst_ref=back.at[pl.ds(DEVS, 8)],
        send_sem=cross_sem.at[2],
        recv_sem=cross_sem.at[3],
        device_id=(down, d),
        device_id_type=MESH,
    )
    own = d // 8
    own_rows = pl.ds(pl.multiple_of(8 * d, 8), ROWS)
    own_message = pltpu.make_async_copy(out_msg.at[own_rows], in_msg.at[own_rows], recv_sem.at[own])
    own_reply = pltpu.make_async_copy(sums.at[pl.ds(d, 1)], back.at[pl.ds(d, 1)], ret_recv_sem)

    def octet(t):
        far = (t + 1) // 2
        shift = jnp.where(t % 2 == 1, far, 8 - far)
        return (own + shift) % 8

    metas[...] = jnp.zeros_like(metas)
    sums[...] = jnp.zeros_like(sums)
    back[TILES:128, :] = jnp.zeros((128 - TILES, 128), f32)
    pl.semaphore_wait(barrier, DEVS + 1)

    def send_octet(t, _):
        base = 8 * octet(8 - t)
        for i in range(8):
            message(base + (d + i) % 8, d).start()
        return 0

    lax.fori_loop(1, 8, send_octet, 0)
    own_message.start()
    for i in range(1, 8):
        message(8 * own + (d + i) % 8, d).start()
    cross_message.start()

    world = []
    for m in range(3):
        p = pose_cols[0:GRAINS, 16 * m + 14 : 16 * m + 15]
        for n in range(3):
            lane_r = 16 * n + 4 * m
            p = p + pose_cols[0:GRAINS, lane_r : lane_r + 1] * coords_ref[n]
        world.append(p)
    ones = jnp.where(iota((GRAINS, NODES), 0) == 0, 1.0, 0.0)
    world = parts(jnp.concatenate(world + [ones], axis=0))
    for combo, part in enumerate(P_PART):
        for block in range(8):
            points[128 * combo + 16 * block : 128 * combo + 16 * block + 16, :] = world[part]
    attr_rows = matmul_nt(attr_b, order)
    lane8 = iota((8, 128), 1)
    lane8_f = lane8 & 15
    per_lane = jnp.where(
        lane8_f < 12, 2.0**-30, jnp.where(lane8_f == 12, 2.0**-27, jnp.where(lane8_f == 13, 2.0**-28 / LEVELS, 0.0))
    )

    def work(t, _):
        is_cross = t == 1
        vg = jnp.where(is_cross, 8, octet(jnp.where(t > 1, 9 - t, 0)))

        @pl.when(is_cross)
        def _():
            cross_message.wait_recv()

        @pl.when(t != 1)
        def _():
            messages(8, vg).wait_recv()

        at = pl.multiple_of(64 * vg, 64)
        meta = in_msg[pl.ds(at + 4, 8, stride=8), :].astype(f32) * per_lane
        metas[pl.ds(pl.multiple_of(8 * vg, 8), 8), :] = meta
        node = [cols[pl.ds(pl.multiple_of(128 * c + 8 * vg, 8), 8), :][:, 4:5] for c in range(2)]
        mine = [jnp.logical_or((lane8 & 3) == node[c].astype(i32) - 1, lane8_f == 12) for c in range(2)]
        left = [
            jnp.where(jnp.logical_and(mine[c], (lane8 >> 4) == 4 * c + k), meta, 0.0) for k in range(3) for c in range(2)
        ]
        left = parts(jnp.concatenate(left, axis=0))
        place = matmul(jnp.concatenate([left[part] for part in R_PART], axis=1), points[...])
        result = jnp.zeros((8, 128), f32)
        for c in range(2):
            even = in_msg[pl.ds(at + 2 * c, 8, stride=8), :]
            odd = in_msg[pl.ds(at + 2 * c + 1, 8, stride=8), :]
            scale = jnp.broadcast_to(jnp.where(node[c] > 0.5, meta[:, 64 * c + 13 : 64 * c + 14], 0.0), (8, 128))
            total = None
            for chunk in range(NODES // 128):
                u = tuple(place[16 * k + 8 * c : 16 * k + 8 * c + 8, 128 * chunk : 128 * chunk + 128] for k in range(3))
                term = contact(even, odd, scale, u)
                total = term if total is None else tuple(a + b for a, b in zip(total, term))
            for n in range(6):
                result = jnp.where(lane8 == 8 * c + n, jnp.sum(total[n], axis=1, keepdims=True), result)
        sums[pl.ds(pl.multiple_of(8 * vg, 8), 8), :] = result

        @pl.when(is_cross)
        def _():
            cross_reply.start()

        @pl.when(t == 0)
        def _():
            own_reply.start()
            for i in range(1, 8):
                reply(8 * vg + (d + i) % 8, d).start()

        @pl.when(t > 1)
        def _():
            for i in range(8):
                reply(8 * vg + (d + i) % 8, d).start()

        return 0

    lax.fori_loop(0, 9, work, 0)

    sums_t = sums[...].T
    lane_p = iota((8, 128), 1)
    row_p = iota((8, 128), 0)

    def per_grain(tables, masks):
        out = jnp.zeros((8, 128), f32)
        for grain in range(GRAINS):
            kept = sum(jnp.where(masks[c] == grain + 1.0, tables[c], 0.0) for c in range(2))
            out = jnp.where(lane_p == grain, jnp.sum(kept, axis=1, keepdims=True), out)
        return out

    def stack(rows):
        out = jnp.zeros((8, 128), f32)
        for n, row in enumerate(rows):
            out = jnp.where(row_p == n, row, out)
        return out

    meta_t = metas[...].T
    node_tables, node_masks = [], []
    for c in range(2):
        at = 64 * c
        r = [[meta_t[at + 16 * k + 4 * m : at + 16 * k + 4 * m + 1, :] for k in range(3)] for m in range(3)]
        mask = attr_rows[4:5, 128 * c : 128 * c + 128]
        centre = []
        for m in range(3):
            value = jnp.zeros((1, 128), f32)
            for grain in range(GRAINS):
                value = jnp.where(mask == grain + 1.0, pose[16 * m + 14 : 16 * m + 15, grain : grain + 1], value)
            centre.append(value)
        shift = [
            r[0][k] * centre[0] + r[1][k] * centre[1] + r[2][k] * centre[2] + meta_t[at + 16 * k + 12 : at + 16 * k + 13, :]
            for k in range(3)
        ]
        push = [sums_t[8 * c + n : 8 * c + n + 1, :] for n in range(3)]
        twist = [sums_t[8 * c + 3 + n : 8 * c + 4 + n, :] for n in range(3)]
        lever = cross(shift, push)
        twist = [twist[n] - lever[n] for n in range(3)]
        rows = [r[m][0] * v[0] + r[m][1] * v[1] + r[m][2] * v[2] for v in (push, twist) for m in range(3)]
        node_tables.append(stack(rows))
        node_masks.append(mask)
    node_load = per_grain(node_tables, node_masks)

    replies(DEVS).wait_recv()
    cross_reply.wait_recv()
    back_t = back[...].T
    grid_tables, grid_masks = [], []
    for c in range(2):
        corner = [((GRID - 1) / 2.0 - BASE) - attr_rows[1 + k : 2 + k, 128 * c : 128 * c + 128] for k in range(3)]
        push = [back_t[8 * c + n : 8 * c + n + 1, :] for n in range(3)]
        lever = cross(corner, push)
        twist = [back_t[8 * c + 3 + n : 8 * c + 4 + n, :] - lever[n] for n in range(3)]
        grid_tables.append(stack(push + twist))
        grid_masks.append(attr_rows[0:1, 128 * c : 128 * c + 128])
    grid_load = per_grain(grid_tables, grid_masks)

    def turn(first):
        v = [grid_load[first + k : first + k + 1, 0:GRAINS] for k in range(3)]
        return [rot[3 * m] * v[0] + rot[3 * m + 1] * v[1] + rot[3 * m + 2] * v[2] for m in range(3)]

    force, torque = turn(0), turn(3)
    force = [node_load[m : m + 1, 0:GRAINS] - force[m] for m in range(3)]
    torque = [node_load[3 + m : 4 + m, 0:GRAINS] - torque[m] for m in range(3)]
    mass = mass_ref[...]
    gain = time_step / mass
    spin_gain = time_step / (0.4 * mass * (3.0 * GRID / 16.0) ** 2)
    vel = [velocity_ref[m : m + 1, :] + force[m] * gain for m in range(3)]
    spin = [spin_ref[m : m + 1, :] + torque[m] * spin_gain for m in range(3)]
    for m in range(3):
        new_velocity_ref[m : m + 1, :] = vel[m]
        new_spin_ref[m : m + 1, :] = spin[m]
        new_position_ref[m : m + 1, :] = pos[m] + time_step * vel[m]
    vec = (x, y, z)
    turned = cross(spin, vec)
    quarter = 0.5 * time_step
    q = [w - quarter * (spin[0] * x + spin[1] * y + spin[2] * z)]
    q += [vec[m] + quarter * (w * spin[m] + turned[m]) for m in range(3)]
    norm = jnp.sqrt(q[0] * q[0] + q[1] * q[1] + q[2] * q[2] + q[3] * q[3])
    for k in range(4):
        new_quaternion_ref[k : k + 1, :] = q[k] / norm

    messages(DEVS - 1, 0).wait_send()
    replies(DEVS - 1).wait_send()
    cross_message.wait_send()
    cross_reply.wait_send()


ROWS = 5
SMALL = 12
SCRATCH = 22


def settle_kernel(*refs):
    sem = refs[8]
    copies = [pltpu.make_async_copy(refs[n], refs[4 + n], sem.at[n]) for n in range(4)]
    for copy in copies:
        copy.start()
    for copy in copies:
        copy.wait()


def settle(outs):
    anywhere = pl.BlockSpec(memory_space=pl.ANY)
    return pl.pallas_call(
        settle_kernel,
        out_shape=[jax.ShapeDtypeStruct(a.shape, a.dtype) for a in outs],
        in_specs=[anywhere] * 4,
        out_specs=[anywhere] * 4,
        scratch_shapes=[pltpu.SemaphoreType.DMA((4,))],
    )(*outs)


def body(
    level_set, node_coords, position, quaternion, velocity, spin, mass, grid_slot, brick_anchor, node_slot, grid_cross,
    anchor_cross, node_cross,
):
    vmem = pl.BlockSpec(memory_space=pltpu.VMEM)
    dma = pltpu.SemaphoreType.DMA
    row = lambda a: a.reshape(1, -1)
    small = (
        node_coords, position, quaternion, velocity, spin, row(mass), row(grid_slot), brick_anchor, row(node_slot),
        row(grid_cross), anchor_cross, row(node_cross),
    )
    outs = pl.pallas_call(
        kernel,
        out_shape=[jax.ShapeDtypeStruct((n, GRAINS), f32) for n in (3, 4, 3, 3)],
        in_specs=[pl.BlockSpec(memory_space=pl.ANY)] * (1 + SMALL),
        out_specs=[vmem] * 4,
        scratch_shapes=[
            pltpu.VMEM((GRAINS, SPAN, 32, GRID), bf16),
            pltpu.VMEM((128, 256), f32),
            pltpu.VMEM((256, 128), f32),
            pltpu.VMEM((384, 128), f32),
            pltpu.VMEM((128, 128), f32),
            pltpu.VMEM((128 * len(P_PART), NODES), bf16),
            pltpu.VMEM((8 * TILES, 128), i32),
            pltpu.VMEM((8 * TILES, 128), i32),
            pltpu.VMEM((128, 128), f32),
            pltpu.VMEM((128, 128), f32),
            pltpu.VMEM((128, 128), f32),
            dma,
            dma,
            dma((8,)),
            dma,
            dma,
            dma((4,)),
            dma((SMALL,)),
        ]
        + [pltpu.VMEM(a.shape, a.dtype) for a in small],
        compiler_params=pltpu.CompilerParams(
            collective_id=0, has_side_effects=True, vmem_limit_bytes=60 * 1024 * 1024
        ),
    )(level_set, *small)
    return tuple(settle(outs))


def solution(mesh):
    both = ("group", "dev")
    wide, flat = P(None, both), P(both)
    in_specs = (
        P(both, None, None, None), P(None, both, None), wide, wide, wide, wide, flat, flat, wide, flat, flat, wide, flat,
    )
    return jax.shard_map(body, mesh=mesh, in_specs=in_specs, out_specs=(wide,) * 4, check_vma=False)
```

```python
import jax
import jax.numpy as jnp
from jax import lax
from jax.experimental import pallas as pl
from jax.experimental.pallas import tpu as pltpu
from jax.sharding import PartitionSpec as P

MESH = pl.DeviceIdType.MESH
f32, bf16, i32 = jnp.float32, jnp.bfloat16, jnp.int32

GRID = 64
GROUPS = 8
DEVS = 64
GRAINS = 4
NODES = 512
BASE = GRID // 2 - 5
SPAN = 10
TILES = DEVS + 8
PAIRS = 2 * TILES
LEVELS = 32766.0
stiffness = 0.1
time_step = 0.5
R_PART = (0, 0, 1, 1)
P_PART = (0, 1, 0, 1)


def iota(shape, dim):
    return lax.broadcasted_iota(i32, shape, dim)


def parts(x):
    first = x.astype(bf16)
    rest = x - first.astype(f32)
    second = rest.astype(bf16)
    third = (rest - second.astype(f32)).astype(bf16)
    return first, second, third


def matmul(a, b):
    return jnp.dot(a, b, preferred_element_type=f32)


def matmul_nt(a, b):
    return lax.dot_general(a, b, (((1,), (1,)), ((), ())), preferred_element_type=f32)


def hat(t):
    return jnp.maximum(1.0 - jnp.abs(t), 0.0)


def slope(t):
    return jnp.maximum(jnp.minimum(-2.0 * t, jnp.maximum(t + 1.5, 0.0)), jnp.minimum(t - 1.5, 0.0))


def take(table, index):
    return jnp.take_along_axis(table, index, axis=1, mode="promise_in_bounds")


def near(u):
    r = jnp.floor(u + 0.5)
    f = u - r
    e = jnp.abs(f)
    up = f >= 0.0
    half = jnp.where(up, 0.5, -0.5)
    step = jnp.where(up, 1, -1)
    a = r.astype(i32)
    b = a + step
    c = a - step
    in_a, in_b, in_c = ((i & -8) == 0 for i in (a, b, c))
    hats = (jnp.where(in_a, 1.0 - e, 0.0), jnp.where(in_b, e, 0.0))
    slopes = (
        jnp.where(in_a, -2.0 * f, 0.0),
        jnp.where(in_b, f + half, 0.0),
        jnp.where(in_c, f - half, 0.0),
    )
    return (a & 7, b & 7, c & 7), hats, slopes


def contact(even, odd, scale, u):
    rx = jnp.floor(u[0] + 0.5).astype(i32)
    bit_e = ((rx + 1) << 4) & 64
    bit_o = ((rx - 1) << 4) & 64
    de = u[0] - (bit_e >> 4).astype(f32)
    do = u[0] - (bit_o >> 4).astype(f32) - 2.0
    tiny = 1.0 / 65536.0

    def lanes(weight):
        hi_e, hi_o = weight(de - 1.0) * tiny, weight(do - 1.0) * tiny
        return weight(de) - hi_e, hi_e, weight(do) - hi_o, hi_o

    hx, sx = lanes(hat), lanes(slope)
    yi, hy, sy = near(u[1])
    zi, hz, sz = near(u[2])
    yi = [i << 3 for i in yi]

    def column(j, k, with_slope):
        place = yi[j] | zi[k]
        we, wo = take(even, bit_e | place), take(odd, bit_o | place)
        values = (((we << 16) >> 16).astype(f32), we.astype(f32), ((wo << 16) >> 16).astype(f32), wo.astype(f32))

        def meet(w):
            return (values[0] * w[0] + values[1] * w[1]) + (values[2] * w[2] + values[3] * w[3])

        return meet(hx), (meet(sx) if with_slope else None)

    rows, rows_x, rows_z = [], [], []
    for j in range(2):
        v0, s0 = column(j, 0, True)
        v1, s1 = column(j, 1, True)
        v2, _ = column(j, 2, False)
        rows.append(v0 * hz[0] + v1 * hz[1])
        rows_x.append(s0 * hz[0] + s1 * hz[1])
        rows_z.append(v0 * sz[0] + v1 * sz[1] + v2 * sz[2])
    v0, _ = column(2, 0, False)
    v1, _ = column(2, 1, False)
    rows.append(v0 * hz[0] + v1 * hz[1])
    phi = (rows[0] * hy[0] + rows[1] * hy[1]) * scale
    gx = (rows_x[0] * hy[0] + rows_x[1] * hy[1]) * scale
    gy = (rows[0] * sy[0] + rows[1] * sy[1] + rows[2] * sy[2]) * scale
    gz = (rows_z[0] * hy[0] + rows_z[1] * hy[1]) * scale
    push = stiffness * jnp.maximum(-phi, 0.0) * lax.rsqrt(jnp.maximum(gx * gx + gy * gy + gz * gz, 1.0))
    g = (gx * push, gy * push, gz * push)
    return g + cross(u, g)


def cross(a, b):
    return (a[1] * b[2] - a[2] * b[1], a[2] * b[0] - a[0] * b[2], a[0] * b[1] - a[1] * b[0])


def kernel(
    level_ref, *refs
):
    sources, refs = refs[:SMALL], refs[SMALL:]
    (
        out_ref,
        window, attr, cols, slab, pose, points, out_msg, in_msg, metas, sums, back,
        window_sem, send_sem, recv_sem, ret_send_sem, ret_recv_sem, cross_sem, input_sem,
    ) = refs[:SCRATCH]
    inputs = refs[SCRATCH:]
    (
        coords_ref, position_ref, quaternion_ref, velocity_ref, spin_ref, mass_ref, grid_ref, anchor_ref, node_ref,
        grid_cross_ref, anchor_cross_ref, node_cross_ref,
    ) = inputs
    g = lax.axis_index("group")
    d = lax.axis_index("dev")
    up, down = lax.rem(g + 1, GROUPS), lax.rem(g + GROUPS - 1, GROUPS)
    barrier = pltpu.get_barrier_semaphore()

    def greet(k, _):
        e = lax.rem(d + k, DEVS)
        pl.semaphore_signal(barrier, inc=1, device_id=(g, e), device_id_type=MESH)
        return 0

    load = pltpu.make_async_copy(
        level_ref.at[:, BASE : BASE + SPAN, 16:48, :], window, window_sem
    )
    load.start()
    fetches = [
        pltpu.make_async_copy(source, target, input_sem.at[n])
        for n, (source, target) in enumerate(zip(sources, inputs))
    ]
    for fetch in fetches:
        fetch.start()
    greet(DEVS // 2, 0)

    def greet_two(j, _):
        greet(DEVS // 2 - j, 0)
        return greet(DEVS // 2 + j, 0)

    lax.fori_loop(1, DEVS // 2, greet_two, 0, unroll=4)
    for other in (up, down):
        pl.semaphore_signal(barrier, inc=1, device_id=(other, d), device_id_type=MESH)

    for fetch in fetches:
        fetch.wait()

    attr[...] = jnp.zeros_like(attr)
    attr[0:1, 0:128] = (grid_ref[...] + 1).astype(f32)
    attr[0:1, 128:144] = (grid_cross_ref[...] + 1).astype(f32)
    attr[1:4, 0:128] = (anchor_ref[...] - BASE).astype(f32)
    attr[1:4, 128:144] = (anchor_cross_ref[...] - BASE).astype(f32)
    attr[4:5, 0:128] = (node_ref[...] + 1).astype(f32)
    attr[4:5, 128:144] = (node_cross_ref[...] + 1).astype(f32)
    slot_to = iota((256, 256), 0)
    order = (iota((256, 256), 1) == ((slot_to & 127) << 1) + (slot_to >> 7)).astype(f32).astype(bf16)
    attr_b = attr[...].astype(bf16)
    cols[...] = matmul_nt(order, attr_b)

    w, x, y, z = (quaternion_ref[k : k + 1, :] for k in range(4))
    rot = (
        1.0 - 2.0 * (y * y + z * z), 2.0 * (x * y - w * z), 2.0 * (x * z + w * y),
        2.0 * (x * y + w * z), 1.0 - 2.0 * (x * x + z * z), 2.0 * (y * z - w * x),
        2.0 * (x * z - w * y), 2.0 * (y * z + w * x), 1.0 - 2.0 * (x * x + y * y),
    )
    pos = [position_ref[m : m + 1, :] for m in range(3)]
    pose[...] = jnp.zeros_like(pose)
    for k in range(3):
        turned = rot[k] * pos[0] + rot[3 + k] * pos[1] + rot[6 + k] * pos[2]
        for half in (0, 64):
            at = half + 16 * k
            for m in range(3):
                pose[at + 4 * m : at + 4 * m + 4, 0:GRAINS] = jnp.broadcast_to(rot[3 * m + k], (4, GRAINS))
            pose[at + 12 : at + 13, 0:GRAINS] = ((GRID - 1) / 2.0 - BASE) - turned
            pose[at + 14 : at + 15, 0:GRAINS] = pos[k]
    pose_cols = pose[...].T

    lane64 = iota((64, 384), 1)
    select_z = (iota((64, 384), 0) == BASE + (lane64 >> 7) + (lane64 & 7)).astype(f32).astype(bf16)
    place_y = iota((16, 128), 0)
    lane_y = (iota((16, 128), 1) >> 3) & 7
    load.wait()
    planes = matmul(window[...].reshape(GRAINS * SPAN * 32, GRID), select_z)
    planes = planes.reshape(GRAINS * SPAN, 32, 384)[:, 8:24, :]
    low_half = iota((40, 128), 1) < 64
    for ay in range(3):
        keep = (place_y == BASE - 24 + ay + lane_y).astype(f32)
        for az in range(3):
            picked = jnp.sum(planes[:, :, 128 * az : 128 * az + 128] * keep[None], axis=1)
            q = 3 * ay + az
            slab[40 * q : 40 * q + 40, :] = jnp.where(low_half, picked, pltpu.roll(picked, 36, 0))
    slab[360:384, :] = jnp.zeros((24, 128), f32)
    code = [
        (cols[128 * c : 128 * c + TILES, 2:3] * 3.0 + cols[128 * c : 128 * c + TILES, 3:4]) * 40.0
        + (cols[128 * c : 128 * c + TILES, 0:1] - 1.0) * 10.0
        + cols[128 * c : 128 * c + TILES, 1:2]
        for c in range(2)
    ]
    code = jnp.concatenate([code[c] + float(j) for c in range(2) for j in range(4)], axis=0).astype(i32)
    pick = (iota((8 * TILES, 384), 1) == code).astype(f32).astype(bf16)
    bricks = matmul(pick, slab[...].astype(bf16))
    lane = iota((TILES, 128), 1)
    pose_parts = parts(pose_cols)
    lane_f = lane & 15
    unit = jnp.where(
        lane_f < 12, 2.0**30, jnp.where(lane_f == 12, 2.0**27, jnp.where(lane_f == 13, 2.0**28, 0.0))
    )
    halves = []
    for c in range(2):
        rows = [bricks[TILES * (4 * c + j) : TILES * (4 * c + j + 1), :] for j in range(4)]
        most = jnp.maximum(
            jnp.maximum(jnp.abs(rows[0]), jnp.abs(rows[1])), jnp.maximum(jnp.abs(rows[2]), jnp.abs(rows[3]))
        )
        most = jnp.maximum(jnp.max(most, axis=1, keepdims=True), 1e-6)
        inverse = LEVELS / most
        level = [jnp.floor(row * inverse + 0.5).astype(i32) for row in rows]
        out_msg[pl.ds(2 * c, TILES, stride=8), :] = (level[1] << 16) + level[0]
        out_msg[pl.ds(2 * c + 1, TILES, stride=8), :] = (level[3] << 16) + level[2]
        own = cols[128 * c : 128 * c + TILES, :]
        grain = (own[:, 0:1].astype(i32) - 1 == lane).astype(f32).astype(bf16)
        meta = matmul(grain, pose_parts[0]) + matmul(grain, pose_parts[1]) + matmul(grain, pose_parts[2])
        for k in range(3):
            meta = meta - jnp.where(lane == 64 * c + 16 * k + 12, own[:, 1 + k : 2 + k], 0.0)
        halves.append(jnp.where(lane_f == 13, most, meta))
    out_msg[pl.ds(4, TILES, stride=8), :] = (jnp.where(lane < 64, halves[0], halves[1]) * unit).astype(i32)

    def message(e, other):
        return pltpu.make_async_remote_copy(
            src_ref=out_msg.at[pl.ds(pl.multiple_of(8 * e, 8), ROWS)],
            dst_ref=in_msg.at[pl.ds(pl.multiple_of(8 * other, 8), ROWS)],
            send_sem=send_sem,
            recv_sem=recv_sem.at[other // 8],
            device_id=(g, e),
            device_id_type=MESH,
        )

    def messages(count, octet):
        return pltpu.make_async_remote_copy(
            src_ref=out_msg.at[pl.ds(0, ROWS * count)],
            dst_ref=in_msg.at[pl.ds(0, ROWS * count)],
            send_sem=send_sem,
            recv_sem=recv_sem.at[octet],
            device_id=(up, d),
            device_id_type=MESH,
        )

    def reply(e, other):
        return pltpu.make_async_remote_copy(
            src_ref=sums.at[pl.ds(e, 1)],
            dst_ref=back.at[pl.ds(other, 1)],
            send_sem=ret_send_sem,
            recv_sem=ret_recv_sem,
            device_id=(g, e),
            device_id_type=MESH,
        )

    def replies(count):
        return pltpu.make_async_remote_copy(
            src_ref=sums.at[pl.ds(0, count)],
            dst_ref=back.at[pl.ds(0, count)],
            send_sem=ret_send_sem,
            recv_sem=ret_recv_sem,
            device_id=(up, d),
            device_id_type=MESH,
        )

    cross_message = pltpu.make_async_remote_copy(
        src_ref=out_msg.at[pl.ds(8 * DEVS, 64)],
        dst_ref=in_msg.at[pl.ds(8 * DEVS, 64)],
        send_sem=cross_sem.at[0],
        recv_sem=cross_sem.at[1],
        device_id=(up, d),
        device_id_type=MESH,
    )
    cross_reply = pltpu.make_async_remote_copy(
        src_ref=sums.at[pl.ds(DEVS, 8)],
        dst_ref=back.at[pl.ds(DEVS, 8)],
        send_sem=cross_sem.at[2],
        recv_sem=cross_sem.at[3],
        device_id=(down, d),
        device_id_type=MESH,
    )
    own = d // 8
    own_rows = pl.ds(pl.multiple_of(8 * d, 8), ROWS)
    own_message = pltpu.make_async_copy(out_msg.at[own_rows], in_msg.at[own_rows], recv_sem.at[own])
    own_reply = pltpu.make_async_copy(sums.at[pl.ds(d, 1)], back.at[pl.ds(d, 1)], ret_recv_sem)

    def octet(t):
        far = (t + 1) // 2
        shift = jnp.where(t % 2 == 1, far, 8 - far)
        return (own + shift) % 8

    metas[...] = jnp.zeros_like(metas)
    sums[...] = jnp.zeros_like(sums)
    back[TILES:128, :] = jnp.zeros((128 - TILES, 128), f32)
    pl.semaphore_wait(barrier, DEVS + 1)

    def send_octet(t, _):
        base = 8 * octet(8 - t)
        for i in range(8):
            message(base + (d + i) % 8, d).start()
        return 0

    lax.fori_loop(1, 8, send_octet, 0)
    own_message.start()
    for i in range(1, 8):
        message(8 * own + (d + i) % 8, d).start()
    cross_message.start()

    world = []
    for m in range(3):
        p = pose_cols[0:GRAINS, 16 * m + 14 : 16 * m + 15]
        for n in range(3):
            lane_r = 16 * n + 4 * m
            p = p + pose_cols[0:GRAINS, lane_r : lane_r + 1] * coords_ref[n]
        world.append(p)
    ones = jnp.where(iota((GRAINS, NODES), 0) == 0, 1.0, 0.0)
    world = parts(jnp.concatenate(world + [ones], axis=0))
    for combo, part in enumerate(P_PART):
        for block in range(8):
            points[128 * combo + 16 * block : 128 * combo + 16 * block + 16, :] = world[part]
    attr_rows = matmul_nt(attr_b, order)
    lane8 = iota((8, 128), 1)
    lane8_f = lane8 & 15
    per_lane = jnp.where(
        lane8_f < 12, 2.0**-30, jnp.where(lane8_f == 12, 2.0**-27, jnp.where(lane8_f == 13, 2.0**-28 / LEVELS, 0.0))
    )

    def work(t, _):
        is_cross = t == 8
        vg = jnp.where(is_cross, 8, octet(jnp.where(t > 0, 8 - t, 0)))

        @pl.when(is_cross)
        def _():
            cross_message.wait_recv()

        @pl.when(t != 8)
        def _():
            messages(8, vg).wait_recv()

        at = pl.multiple_of(64 * vg, 64)
        meta = in_msg[pl.ds(at + 4, 8, stride=8), :].astype(f32) * per_lane
        metas[pl.ds(pl.multiple_of(8 * vg, 8), 8), :] = meta
        node = [cols[pl.ds(pl.multiple_of(128 * c + 8 * vg, 8), 8), :][:, 4:5] for c in range(2)]
        mine = [jnp.logical_or((lane8 & 3) == node[c].astype(i32) - 1, lane8_f == 12) for c in range(2)]
        left = [
            jnp.where(jnp.logical_and(mine[c], (lane8 >> 4) == 4 * c + k), meta, 0.0) for k in range(3) for c in range(2)
        ]
        left = parts(jnp.concatenate(left, axis=0))
        place = matmul(jnp.concatenate([left[part] for part in R_PART], axis=1), points[...])
        result = jnp.zeros((8, 128), f32)
        for c in range(2):
            even = in_msg[pl.ds(at + 2 * c, 8, stride=8), :]
            odd = in_msg[pl.ds(at + 2 * c + 1, 8, stride=8), :]
            scale = jnp.broadcast_to(jnp.where(node[c] > 0.5, meta[:, 64 * c + 13 : 64 * c + 14], 0.0), (8, 128))
            total = None
            for chunk in range(NODES // 128):
                u = tuple(place[16 * k + 8 * c : 16 * k + 8 * c + 8, 128 * chunk : 128 * chunk + 128] for k in range(3))
                term = contact(even, odd, scale, u)
                total = term if total is None else tuple(a + b for a, b in zip(total, term))
            for n in range(6):
                result = jnp.where(lane8 == 8 * c + n, jnp.sum(total[n], axis=1, keepdims=True), result)
        sums[pl.ds(pl.multiple_of(8 * vg, 8), 8), :] = result

        @pl.when(is_cross)
        def _():
            cross_reply.start()

        @pl.when(t == 0)
        def _():
            own_reply.start()
            for i in range(1, 8):
                reply(8 * vg + (d + i) % 8, d).start()

        @pl.when(jnp.logical_and(t > 0, t < 8))
        def _():
            for i in range(8):
                reply(8 * vg + (d + i) % 8, d).start()

        return 0

    lax.fori_loop(0, 9, work, 0)

    sums_t = sums[...].T
    lane_p = iota((8, 128), 1)
    row_p = iota((8, 128), 0)

    def per_grain(tables, masks):
        out = jnp.zeros((8, 128), f32)
        for grain in range(GRAINS):
            kept = sum(jnp.where(masks[c] == grain + 1.0, tables[c], 0.0) for c in range(2))
            out = jnp.where(lane_p == grain, jnp.sum(kept, axis=1, keepdims=True), out)
        return out

    def stack(rows):
        out = jnp.zeros((8, 128), f32)
        for n, row in enumerate(rows):
            out = jnp.where(row_p == n, row, out)
        return out

    meta_t = metas[...].T
    node_tables, node_masks = [], []
    for c in range(2):
        at = 64 * c
        r = [[meta_t[at + 16 * k + 4 * m : at + 16 * k + 4 * m + 1, :] for k in range(3)] for m in range(3)]
        mask = attr_rows[4:5, 128 * c : 128 * c + 128]
        centre = []
        for m in range(3):
            value = jnp.zeros((1, 128), f32)
            for grain in range(GRAINS):
                value = jnp.where(mask == grain + 1.0, pose[16 * m + 14 : 16 * m + 15, grain : grain + 1], value)
            centre.append(value)
        shift = [
            r[0][k] * centre[0] + r[1][k] * centre[1] + r[2][k] * centre[2] + meta_t[at + 16 * k + 12 : at + 16 * k + 13, :]
            for k in range(3)
        ]
        push = [sums_t[8 * c + n : 8 * c + n + 1, :] for n in range(3)]
        twist = [sums_t[8 * c + 3 + n : 8 * c + 4 + n, :] for n in range(3)]
        lever = cross(shift, push)
        twist = [twist[n] - lever[n] for n in range(3)]
        rows = [r[m][0] * v[0] + r[m][1] * v[1] + r[m][2] * v[2] for v in (push, twist) for m in range(3)]
        node_tables.append(stack(rows))
        node_masks.append(mask)
    node_load = per_grain(node_tables, node_masks)

    replies(DEVS).wait_recv()
    cross_reply.wait_recv()
    back_t = back[...].T
    grid_tables, grid_masks = [], []
    for c in range(2):
        corner = [((GRID - 1) / 2.0 - BASE) - attr_rows[1 + k : 2 + k, 128 * c : 128 * c + 128] for k in range(3)]
        push = [back_t[8 * c + n : 8 * c + n + 1, :] for n in range(3)]
        lever = cross(corner, push)
        twist = [back_t[8 * c + 3 + n : 8 * c + 4 + n, :] - lever[n] for n in range(3)]
        grid_tables.append(stack(push + twist))
        grid_masks.append(attr_rows[0:1, 128 * c : 128 * c + 128])
    grid_load = per_grain(grid_tables, grid_masks)

    def turn(first):
        v = [grid_load[first + k : first + k + 1, 0:GRAINS] for k in range(3)]
        return [rot[3 * m] * v[0] + rot[3 * m + 1] * v[1] + rot[3 * m + 2] * v[2] for m in range(3)]

    force, torque = turn(0), turn(3)
    force = [node_load[m : m + 1, 0:GRAINS] - force[m] for m in range(3)]
    torque = [node_load[3 + m : 4 + m, 0:GRAINS] - torque[m] for m in range(3)]
    mass = mass_ref[...]
    gain = time_step / mass
    spin_gain = time_step / (0.4 * mass * (3.0 * GRID / 16.0) ** 2)
    vel = [velocity_ref[m : m + 1, :] + force[m] * gain for m in range(3)]
    spin = [spin_ref[m : m + 1, :] + torque[m] * spin_gain for m in range(3)]
    out_ref[...] = jnp.zeros_like(out_ref)
    for m in range(3):
        out_ref[2, m : m + 1, :] = vel[m]
        out_ref[3, m : m + 1, :] = spin[m]
        out_ref[0, m : m + 1, :] = pos[m] + time_step * vel[m]
    vec = (x, y, z)
    turned = cross(spin, vec)
    quarter = 0.5 * time_step
    q = [w - quarter * (spin[0] * x + spin[1] * y + spin[2] * z)]
    q += [vec[m] + quarter * (w * spin[m] + turned[m]) for m in range(3)]
    norm = jnp.sqrt(q[0] * q[0] + q[1] * q[1] + q[2] * q[2] + q[3] * q[3])
    for k in range(4):
        out_ref[1, k : k + 1, :] = q[k] / norm

    messages(DEVS - 1, 0).wait_send()
    replies(DEVS - 1).wait_send()
    cross_message.wait_send()
    cross_reply.wait_send()


ROWS = 5
SMALL = 12
SCRATCH = 19


OUT_ROWS = (3, 4, 3, 3)


def settle_kernel(packed, *refs):
    sem = refs[4]
    copies = [
        pltpu.make_async_copy(packed.at[n, pl.ds(0, rows)], refs[n], sem.at[n]) for n, rows in enumerate(OUT_ROWS)
    ]
    for copy in copies:
        copy.start()
    for copy in copies:
        copy.wait()


def settle(packed):
    anywhere = pl.BlockSpec(memory_space=pl.ANY)
    return pl.pallas_call(
        settle_kernel,
        out_shape=[jax.ShapeDtypeStruct((rows, GRAINS), f32) for rows in OUT_ROWS],
        in_specs=[anywhere],
        out_specs=[anywhere] * 4,
        scratch_shapes=[pltpu.SemaphoreType.DMA((4,))],
    )(packed)


def body(
    level_set, node_coords, position, quaternion, velocity, spin, mass, grid_slot, brick_anchor, node_slot, grid_cross,
    anchor_cross, node_cross,
):
    vmem = pl.BlockSpec(memory_space=pltpu.VMEM)
    dma = pltpu.SemaphoreType.DMA
    row = lambda a: a.reshape(1, -1)
    small = (
        node_coords, position, quaternion, velocity, spin, row(mass), row(grid_slot), brick_anchor, row(node_slot),
        row(grid_cross), anchor_cross, row(node_cross),
    )
    outs = pl.pallas_call(
        kernel,
        out_shape=jax.ShapeDtypeStruct((4, 4, GRAINS), f32),
        in_specs=[pl.BlockSpec(memory_space=pl.ANY)] * (1 + SMALL),
        out_specs=vmem,
        scratch_shapes=[
            pltpu.VMEM((GRAINS, SPAN, 32, GRID), bf16),
            pltpu.VMEM((128, 256), f32),
            pltpu.VMEM((256, 128), f32),
            pltpu.VMEM((384, 128), f32),
            pltpu.VMEM((128, 128), f32),
            pltpu.VMEM((128 * len(P_PART), NODES), bf16),
            pltpu.VMEM((8 * TILES, 128), i32),
            pltpu.VMEM((8 * TILES, 128), i32),
            pltpu.VMEM((128, 128), f32),
            pltpu.VMEM((128, 128), f32),
            pltpu.VMEM((128, 128), f32),
            dma,
            dma,
            dma((8,)),
            dma,
            dma,
            dma((4,)),
            dma((SMALL,)),
        ]
        + [pltpu.VMEM(a.shape, a.dtype) for a in small],
        compiler_params=pltpu.CompilerParams(
            collective_id=0, has_side_effects=True, vmem_limit_bytes=60 * 1024 * 1024
        ),
    )(level_set, *small)
    return tuple(settle(outs))


def solution(mesh):
    both = ("group", "dev")
    wide, flat = P(None, both), P(both)
    in_specs = (
        P(both, None, None, None), P(None, both, None), wide, wide, wide, wide, flat, flat, wide, flat, flat, wide, flat,
    )
    return jax.shard_map(body, mesh=mesh, in_specs=in_specs, out_specs=(wide,) * 4, check_vma=False)
```
